256 devices in a mesh: emit: 16 (over x, y_hi, core), recv: 16 (over z, y_lo).
Axes of the slice: x: 4, y: 4 (y_hi: 2, y_lo: 2; y = y_hi * 2 + y_lo), z: 8, core: 2. Of those that a mesh axis runs over, the one named last changes fastest.
Arguments:
- features: bfloat16 [16, 2048, 256], P('emit', 'recv'), may hold values from -6 to 6
- cotangent: bfloat16 [16, 2048, 256], P('recv', 'emit'), may hold values from -6 to 6
- w_msg: bfloat16 [256, 256], replicated, may hold values from -0.375 to 0.375
- w_out: bfloat16 [256, 256], replicated, may hold values from -0.375 to 0.375
- tile_vals: bfloat16 [16, 16, 64, 256, 256], P('emit', 'recv'), may hold values from -0.1875 to 0.1875
- tile_emit: int32 [16, 16, 64], P('emit', 'recv'), may hold values from 0 to 7
- tile_recv: int32 [16, 16, 64], P('emit', 'recv'), may hold values from 0 to 7
- tile_count: int32 [16, 16], P('emit', 'recv'), may hold values from 1 to 64, as said below
Outputs:
- grad_features: bfloat16 [16, 2048, 256], P('emit', 'recv')
- grad_w_msg: float32 [256, 256], replicated
- grad_w_out: float32 [256, 256], replicated
The draws below stay inside these ranges and needn't reach their ends.
Inputs may be any that keep to these rules, and one draw needn't show every extreme that they name: Slots at or beyond a pair's tile_count are unused; some pair holds exactly 64 live slots.
All inputs are finite; a program needn't handle non-finite values.
Results may differ from the reference program's by a relative error of at most 0.034.
Values may be sent and summed in bfloat16 or wider, within the bound.
No kernel may reach another device: no remote copies, remote signals or barrier semaphores. Data moves between devices by JAX's collectives and lax.ppermute only.
A program may use at most 64 MiB of HBM per device.

```python
import jax
import jax.numpy as jnp
from jax import lax

WIDTH = 256
TILE = 256
TILES_DEV = 64
EMIT_GROUPS = 16
RECV_GROUPS = 16
EROWS = 2048
RROWS = 2048
EBLK = 8
RBLK = 8


def draw_tile_count(key, part):
    key = jax.random.fold_in(key, 11)
    key_list = jax.random.split(key, 4)
    grid_shape = (EMIT_GROUPS, RECV_GROUPS)
    first_draw = jax.random.randint(key_list[0], grid_shape, 1, TILES_DEV + 1)
    second_draw = jax.random.randint(key_list[1], grid_shape, 1, TILES_DEV + 1)
    third_draw = jax.random.randint(key_list[2], grid_shape, 1, TILES_DEV + 1)
    smallest = jnp.minimum(jnp.minimum(first_draw, second_draw), third_draw)
    position = jax.random.randint(key_list[3], (), 0, EMIT_GROUPS * RECV_GROUPS)
    flat_index = jnp.arange(EMIT_GROUPS * RECV_GROUPS, dtype=jnp.int32).reshape(grid_shape)
    return jnp.where(flat_index == position, TILES_DEV, smallest).astype(jnp.int32)


def plant(array, stream_key, least, largest):
    shape = array.shape
    index_at = [jax.random.randint(jax.random.fold_in(stream_key, axis), (), 0, shape[axis]) for axis in range(len(shape))]
    array = array.at[tuple(index_at)].set(least)
    longest = shape.index(max(shape))
    index_at[longest] = (index_at[longest] + 1) % shape[longest]
    return array.at[tuple(index_at)].set(largest)


def levels(own_key, extent, shards, low, largest):
    gain = 1.0
    for axis_at, parts in shards:
        steps = jax.random.uniform(jax.random.fold_in(jax.random.fold_in(own_key, 6), axis_at), (parts,), jnp.float32, low / len(shards), largest / len(shards))
        gain = gain * jnp.repeat(jnp.exp(steps), extent[axis_at] // parts).reshape((-1,) + (1,) * (len(extent) - 1 - axis_at))
    return gain


def noise(rng, dims, scale, limit, shards=(), kind=jnp.bfloat16):
    drawn = scale * jax.random.normal(rng, dims, jnp.float32)
    if shards:
        drawn = drawn * levels(rng, dims, shards, -0.22, 0.18)
    return jnp.clip(drawn, -limit, limit).astype(kind)


def setup_inputs(seed: int = 0) -> dict:
    seeds = jax.random.split(jax.random.key(seed), 9)
    return {
        "features": noise(seeds[0], (EMIT_GROUPS, EROWS, WIDTH), 1.0, 6.0, ((0, 16), (1, 16))),
        "cotangent": noise(seeds[1], (RECV_GROUPS, RROWS, WIDTH), 1.0, 6.0, ((0, 16), (1, 16))),
        "w_msg": noise(seeds[2], (WIDTH, WIDTH), WIDTH ** -0.5, 0.375),
        "w_out": noise(seeds[3], (WIDTH, WIDTH), WIDTH ** -0.5, 0.375),
        "tile_vals": noise(seeds[4], (EMIT_GROUPS, RECV_GROUPS, TILES_DEV, TILE, TILE), (4 * TILE) ** -0.5, 0.1875, ((0, 16), (1, 16))),
        "tile_emit": plant(jax.random.randint(seeds[5], (EMIT_GROUPS, RECV_GROUPS, TILES_DEV), 0, EBLK), jax.random.fold_in(seeds[5], 1), 0, EBLK - 1).astype(jnp.int32),
        "tile_recv": plant(jax.random.randint(seeds[6], (EMIT_GROUPS, RECV_GROUPS, TILES_DEV), 0, RBLK), jax.random.fold_in(seeds[6], 1), 0, RBLK - 1).astype(jnp.int32),
        "tile_count": draw_tile_count(jax.random.fold_in(seeds[8], 71), 0),
    }


def reference(features, cotangent, w_msg, w_out, tile_vals, tile_emit, tile_recv, tile_count):
    emitted = jnp.dot(features.reshape(EMIT_GROUPS * EROWS, WIDTH), w_msg, preferred_element_type=jnp.float32)
    emitted = emitted.astype(jnp.bfloat16).reshape(EMIT_GROUPS, EBLK, TILE, WIDTH)

    def forward_partial(emit_index, recv_index):
        def advance(tile_slot, running):
            product = jnp.dot(tile_vals[emit_index, recv_index, tile_slot], emitted[emit_index, tile_emit[emit_index, recv_index, tile_slot]], preferred_element_type=jnp.float32)
            return running.at[tile_recv[emit_index, recv_index, tile_slot]].add(product)

        running = lax.fori_loop(jnp.int32(0), tile_count[emit_index, recv_index], advance, jnp.zeros((RBLK, TILE, WIDTH), jnp.float32))
        rounded = lax.optimization_barrier(running.astype(jnp.bfloat16))
        return rounded.astype(jnp.float32)

    def per_receiver(recv_index):
        def over_emit(running, emit_index):
            return running + forward_partial(emit_index, recv_index), None

        running, unused = lax.scan(over_emit, jnp.zeros((RBLK, TILE, WIDTH), jnp.float32), jnp.arange(EMIT_GROUPS, dtype=jnp.int32))
        return running.reshape(RROWS, WIDTH)

    message = lax.map(per_receiver, jnp.arange(RECV_GROUPS, dtype=jnp.int32))
    message_b = message.reshape(RECV_GROUPS * RROWS, WIDTH).astype(jnp.bfloat16)
    preact = jnp.dot(message_b, w_out, preferred_element_type=jnp.float32)
    sigmoid_pre = jax.nn.sigmoid(preact)
    slope = sigmoid_pre * (1.0 + preact * (1.0 - sigmoid_pre))
    grad_preact = (cotangent.reshape(RECV_GROUPS * RROWS, WIDTH).astype(jnp.float32) * slope).astype(jnp.bfloat16)
    grad_w_out = jnp.dot(message_b.T, grad_preact, preferred_element_type=jnp.float32)
    grad_message = jnp.dot(grad_preact, w_out.T, preferred_element_type=jnp.float32).astype(jnp.bfloat16)
    grad_message = grad_message.reshape(RECV_GROUPS, RBLK, TILE, WIDTH)

    def backward_partial(emit_index, recv_index):
        def advance(tile_slot, running):
            product = jnp.dot(tile_vals[emit_index, recv_index, tile_slot].T, grad_message[recv_index, tile_recv[emit_index, recv_index, tile_slot]], preferred_element_type=jnp.float32)
            return running.at[tile_emit[emit_index, recv_index, tile_slot]].add(product)

        running = lax.fori_loop(jnp.int32(0), tile_count[emit_index, recv_index], advance, jnp.zeros((EBLK, TILE, WIDTH), jnp.float32))
        rounded = lax.optimization_barrier(running.astype(jnp.bfloat16))
        return rounded.astype(jnp.float32)

    def per_emitter(emit_index):
        def over_recv(running, recv_index):
            return running + backward_partial(emit_index, recv_index), None

        running, unused = lax.scan(over_recv, jnp.zeros((EBLK, TILE, WIDTH), jnp.float32), jnp.arange(RECV_GROUPS, dtype=jnp.int32))
        return running.reshape(EROWS, WIDTH)

    grad_emitted = lax.map(per_emitter, jnp.arange(EMIT_GROUPS, dtype=jnp.int32))
    grad_emitted = grad_emitted.reshape(EMIT_GROUPS * EROWS, WIDTH).astype(jnp.bfloat16)
    grad_w_msg = jnp.dot(features.reshape(EMIT_GROUPS * EROWS, WIDTH).T, grad_emitted, preferred_element_type=jnp.float32)
    grad_features = jnp.dot(grad_emitted, w_msg.T, preferred_element_type=jnp.float32).astype(jnp.bfloat16)
    return grad_features.reshape(EMIT_GROUPS, EROWS, WIDTH), grad_w_msg, grad_w_out
```

```python
import functools

import jax
import jax.numpy as jnp
from jax import lax
from jax.experimental import pallas as pl
from jax.experimental.pallas import tpu as pltpu
from jax.sharding import PartitionSpec as P

ring_depth = 16
f32 = jnp.float32
bf16 = jnp.bfloat16


def stream_tiles(live, tiles, ring, sems, consume):
    def copy(slot):
        place = lax.rem(slot, ring_depth)
        return pltpu.make_async_copy(tiles.at[slot], ring.at[place], sems.at[place])

    def begin(slot, carry):
        copy(slot).start()
        return carry

    lax.fori_loop(0, jnp.minimum(live, ring_depth), begin, 0)

    def step(slot, carry):
        copy(slot).wait()
        consume(slot, ring[lax.rem(slot, ring_depth)])

        @pl.when(slot + ring_depth < live)
        def _():
            copy(slot + ring_depth).start()

        return carry

    return lax.fori_loop(0, live, step, 0)


def forward_kernel(source, target, live, core, rows, tiles, kept, sent, acc, ring, sems):
    half = kept.shape[1]
    acc[...] = jnp.zeros_like(acc)

    def consume(slot, tile):
        block = target[slot]
        acc[block] += jnp.dot(tile, rows[source[slot]], preferred_element_type=f32)

    stream_tiles(live[0], tiles, ring, sems, consume)
    own = pl.multiple_of(core[0] * half, half)
    other = pl.multiple_of((1 - core[0]) * half, half)
    for block in range(acc.shape[0]):
        sent[block] = acc[block, pl.ds(other, half), :].astype(bf16)
        kept[block] = acc[block, pl.ds(own, half), :]


def middle_kernel(terms, cotangent, w_msg, w_out, payload):
    width = w_msg.shape[0]
    pieces = terms.shape[0]
    lanes = width // 2
    summed = terms[0].astype(f32)
    for piece in range(1, pieces):
        summed += terms[piece].astype(f32)
    summed = summed.astype(bf16)
    message = jnp.dot(summed, w_msg[...], preferred_element_type=f32).astype(bf16)
    preact = jnp.dot(message, w_out[...], preferred_element_type=f32)
    sigmoid_pre = jax.nn.sigmoid(preact)
    slope = sigmoid_pre * (1.0 + preact * (1.0 - sigmoid_pre))
    grad_preact = (cotangent[...].astype(f32) * slope).astype(bf16)
    across = (((1,), (1,)), ((), ()))
    along = (((0,), (0,)), ((), ()))
    grad_turned = lax.dot_general(w_out[...], grad_preact, across, preferred_element_type=f32).astype(bf16)
    grad = lax.dot_general(grad_preact, w_out[...], across, preferred_element_type=f32).astype(bf16)
    out_part = lax.dot_general(message, grad_preact, along, preferred_element_type=f32).astype(bf16)
    msg_part = lax.dot_general(summed, grad, along, preferred_element_type=f32).astype(bf16)
    parts = (
        out_part[:, :lanes],
        out_part[:, lanes:],
        msg_part[:, :lanes],
        msg_part[:, lanes:],
    )
    chunk = 4 * width // pieces
    for piece in range(pieces):
        payload[piece, :width, :] = grad_turned
        at = 0
        while at < chunk:
            quarter, row = divmod(piece * chunk + at, width)
            size = min(chunk - at, width - row)
            payload[piece, width + at : width + at + size, :] = parts[quarter][row : row + size]
            at += size


def backward_kernel(
    source, target, live, core, held, other, tiles, payload, grads, acc, ring, sems
):
    width, lanes = acc.shape[1], held.shape[2]
    blocks = acc.shape[0]
    acc[...] = jnp.zeros_like(acc)
    chunk = (held.shape[1] - width) // 2

    def place(first, second):
        for block in range(held.shape[0]):
            grads[block, :, :lanes] = first[block, :width, :]
            grads[block, :, lanes:] = second[block, :width, :]

    @pl.when(core[0] == 0)
    def _():
        place(held, other)

    @pl.when(core[0] == 1)
    def _():
        place(other, held)

    def consume(slot, tile):
        block = target[slot]
        acc[block] += jnp.dot(grads[source[slot]], tile, preferred_element_type=f32)

    stream_tiles(live[0], tiles, ring, sems, consume)
    own = pl.ds(pl.multiple_of(width + core[0] * chunk, chunk), chunk)
    weights = held[0, own, :].astype(f32) + other[0, own, :].astype(f32)
    for block in range(1, held.shape[0]):
        weights += held[block, own, :].astype(f32) + other[block, own, :].astype(f32)
    weights = weights.astype(bf16)
    for block in range(blocks):
        for part in range(width // lanes):
            piece = block * (width // lanes) + part
            payload[piece, :width, :] = acc[block, :, part * lanes : (part + 1) * lanes].astype(bf16)
            payload[piece, width:, :] = weights


def weights_kernel(terms, total):
    width = terms.shape[1] - total.shape[1]
    summed = terms[0, width:, :].astype(f32)
    for piece in range(1, terms.shape[0]):
        summed += terms[piece, width:, :].astype(f32)
    for piece in range(total.shape[0]):
        total[piece] = summed


def features_kernel(terms, w_msg, grad):
    width = w_msg.shape[0]
    summed = terms[0, :width, :].astype(f32)
    for piece in range(1, terms.shape[0]):
        summed += terms[piece, :width, :].astype(f32)
    grad[...] = lax.dot_general(
        summed.astype(bf16), w_msg[...], (((0,), (1,)), ((), ())), preferred_element_type=f32
    ).astype(bf16)


def in_vmem(count):
    return [pl.BlockSpec(memory_space=pltpu.VMEM)] * count


def in_smem(count):
    return [pl.BlockSpec(memory_space=pltpu.SMEM)] * count


def limits(mebibytes):
    return pltpu.CompilerParams(vmem_limit_bytes=mebibytes * 2**20)


def per_device(features, cotangent, w_msg, w_out, tile_vals, tile_emit, tile_recv, tile_count):
    own_rows = features[0]
    facet_rows, width = own_rows.shape
    tile_dim = tile_vals.shape[-1]
    emit_size = lax.axis_size("emit")
    recv_size = lax.axis_size("recv")
    recv_blocks = facet_rows * emit_size // tile_dim
    emit_blocks = facet_rows * recv_size // tile_dim
    chips = emit_size // 2
    lanes = width // 2
    values = tile_vals[0, 0]
    emit_slots = tile_emit[0, 0]
    recv_slots = tile_recv[0, 0]
    live = tile_count[0]
    core = lax.rem(lax.axis_index("emit"), 2)[None]
    same_core = [list(range(parity, emit_size, 2)) for parity in range(2)]
    swap = [(member, member ^ 1) for member in range(emit_size)]
    struct = jax.ShapeDtypeStruct
    any_space = pl.BlockSpec(memory_space=pl.ANY)
    sweep_scratch = [
        pltpu.VMEM((ring_depth, tile_dim, tile_dim), bf16),
        pltpu.SemaphoreType.DMA((ring_depth,)),
    ]

    group_rows = lax.all_to_all(
        jnp.broadcast_to(own_rows[None], (recv_size, facet_rows, width)), "recv", 0, 0, tiled=True
    )
    kept, sent = pl.pallas_call(
        forward_kernel,
        out_shape=(
            struct((recv_blocks, tile_dim // 2, width), f32),
            struct((recv_blocks, tile_dim // 2, width), bf16),
        ),
        in_specs=in_smem(4) + in_vmem(1) + [any_space],
        out_specs=tuple(in_vmem(2)),
        scratch_shapes=[pltpu.VMEM((recv_blocks, tile_dim, width), f32)] + sweep_scratch,
        compiler_params=limits(16),
        name="forward_sweep",
    )(emit_slots, recv_slots, live, core, group_rows.reshape(emit_blocks, tile_dim, width), values)
    arrived = lax.ppermute(sent, "emit", swap)
    pair_sum = (kept + arrived.astype(f32)).astype(bf16)
    terms = lax.all_to_all(pair_sum, "emit", 0, 0, tiled=True, axis_index_groups=same_core)

    chunk = 4 * width // chips
    payload = pl.pallas_call(
        middle_kernel,
        out_shape=struct((chips, width + chunk, lanes), bf16),
        in_specs=in_vmem(4),
        out_specs=in_vmem(1)[0],
        compiler_params=limits(16),
        name="middle",
    )(terms, cotangent[0], w_msg, w_out)
    held = lax.all_to_all(payload, "emit", 0, 0, tiled=True, axis_index_groups=same_core)
    other = lax.ppermute(held, "emit", swap)

    back = pl.pallas_call(
        backward_kernel,
        out_shape=struct((recv_size, width + chunk // 2, lanes), bf16),
        in_specs=in_smem(4) + in_vmem(2) + [any_space],
        out_specs=in_vmem(1)[0],
        scratch_shapes=[
            pltpu.VMEM((recv_blocks, width, tile_dim), bf16),
            pltpu.VMEM((emit_blocks, width, tile_dim), f32),
        ]
        + sweep_scratch,
        compiler_params=limits(16),
        name="backward_sweep",
    )(recv_slots, emit_slots, live, core, held, other, values)
    back_terms = lax.all_to_all(back, "recv", 0, 0, tiled=True)

    total = pl.pallas_call(
        weights_kernel,
        out_shape=struct((emit_size, chunk // 2, lanes), f32),
        in_specs=in_vmem(1),
        out_specs=in_vmem(1)[0],
        compiler_params=limits(8),
        name="weights_sum",
    )(back_terms)
    gathered = lax.all_to_all(total, "emit", 0, 0, tiled=True).reshape(4, width, lanes)
    grad_features = pl.pallas_call(
        features_kernel,
        out_shape=struct((facet_rows, width), bf16),
        in_specs=in_vmem(2),
        out_specs=in_vmem(1)[0],
        compiler_params=limits(8),
        name="features_grad",
    )(back_terms, w_msg)[None]
    grad_w_out = jnp.concatenate([gathered[0], gathered[1]], axis=1)
    grad_w_msg = jnp.concatenate([gathered[2], gathered[3]], axis=1)
    return (grad_features, grad_w_msg, grad_w_out)


def solution(mesh):
    in_specs = (
        P("emit", "recv", None),
        P("recv", "emit", None),
        P(),
        P(),
        P("emit", "recv", None, None, None),
        P("emit", "recv", None),
        P("emit", "recv", None),
        P("emit", "recv"),
    )
    out_specs = (P("emit", "recv", None), P(), P())
    return jax.shard_map(
        per_device, mesh=mesh, in_specs=in_specs, out_specs=out_specs, check_vma=False
    )
```

```python
import functools

import jax
import jax.numpy as jnp
from jax import lax
from jax.experimental import pallas as pl
from jax.experimental.pallas import tpu as pltpu
from jax.sharding import PartitionSpec as P

ring_depth = 8
group_tiles = 8
f32 = jnp.float32
bf16 = jnp.bfloat16


def add_group(first, live, tiles, product, target, acc):
    spare = acc.shape[0] - 1
    slots = [first + at for at in range(group_tiles)]
    products = [product(slot, tiles[at]) for at, slot in enumerate(slots)]
    for slot, term in zip(slots, products):
        acc[jnp.where(slot < live, target[slot], spare)] += term


def forward_kernel(source, target, live, core, rows, tiles, kept, sent, acc, ring, sems):
    half = kept.shape[1]
    depth = ring.shape[0]
    steps = lax.div(live[0] + group_tiles - 1, group_tiles)

    def copy(step):
        place = lax.rem(step, depth)
        return pltpu.make_async_copy(
            tiles.at[pl.ds(step * group_tiles, group_tiles)], ring.at[place], sems.at[place]
        )

    def begin(step, carry):
        copy(step).start()
        return carry

    lax.fori_loop(0, jnp.minimum(steps, depth), begin, 0)
    acc[...] = jnp.zeros_like(acc)

    def product(slot, tile):
        return jnp.dot(tile, rows[source[slot]], preferred_element_type=f32)

    def advance(step, carry):
        copy(step).wait()
        held = ring.at[lax.rem(step, depth)]
        add_group(step * group_tiles, live[0], held, product, target, acc)

        @pl.when(step + depth < steps)
        def _():
            copy(step + depth).start()

        return carry

    lax.fori_loop(0, steps, advance, 0)
    own = pl.multiple_of(core[0] * half, half)
    other = pl.multiple_of((1 - core[0]) * half, half)
    for block in range(kept.shape[0]):
        sent[block] = acc[block, pl.ds(other, half), :].astype(bf16)
        kept[block] = acc[block, pl.ds(own, half), :]


def middle_kernel(terms, cotangent, w_msg, w_out, payload):
    width = w_msg.shape[0]
    pieces = terms.shape[0]
    lanes = width // 2
    summed = terms[0].astype(f32)
    for piece in range(1, pieces):
        summed += terms[piece].astype(f32)
    summed = summed.astype(bf16)
    message = jnp.dot(summed, w_msg[...], preferred_element_type=f32).astype(bf16)
    preact = jnp.dot(message, w_out[...], preferred_element_type=f32)
    sigmoid_pre = jax.nn.sigmoid(preact)
    slope = sigmoid_pre * (1.0 + preact * (1.0 - sigmoid_pre))
    grad_preact = (cotangent[...].astype(f32) * slope).astype(bf16)
    across = (((1,), (1,)), ((), ()))
    along = (((0,), (0,)), ((), ()))
    grad_turned = lax.dot_general(w_out[...], grad_preact, across, preferred_element_type=f32).astype(bf16)
    grad = lax.dot_general(grad_preact, w_out[...], across, preferred_element_type=f32).astype(bf16)
    out_part = lax.dot_general(message, grad_preact, along, preferred_element_type=f32).astype(bf16)
    msg_part = lax.dot_general(summed, grad, along, preferred_element_type=f32).astype(bf16)
    parts = (
        out_part[:, :lanes],
        out_part[:, lanes:],
        msg_part[:, :lanes],
        msg_part[:, lanes:],
    )
    chunk = 4 * width // pieces
    for piece in range(pieces):
        payload[piece, :width, :] = grad_turned
        at = 0
        while at < chunk:
            quarter, row = divmod(piece * chunk + at, width)
            size = min(chunk - at, width - row)
            payload[piece, width + at : width + at + size, :] = parts[quarter][row : row + size]
            at += size


def backward_kernel(
    source, target, live, core, held, other, tiles, payload, grads, acc
):
    width, lanes = acc.shape[1], held.shape[2]
    blocks = acc.shape[0] - 1
    chunk = (held.shape[1] - width) // 2

    def place(first, second):
        for block in range(held.shape[0]):
            grads[block, :, :lanes] = first[block, :width, :]
            grads[block, :, lanes:] = second[block, :width, :]

    @pl.when(core[0] == 0)
    def _():
        place(held, other)

    @pl.when(core[0] == 1)
    def _():
        place(other, held)

    acc[...] = jnp.zeros_like(acc)

    def product(slot, tile):
        return jnp.dot(grads[source[slot]], tile, preferred_element_type=f32)

    def advance(step, carry):
        first = step * group_tiles
        add_group(first, live[0], tiles.at[pl.ds(first, group_tiles)], product, target, acc)
        return carry

    lax.fori_loop(0, lax.div(live[0] + group_tiles - 1, group_tiles), advance, 0)
    own = pl.ds(pl.multiple_of(width + core[0] * chunk, chunk), chunk)
    weights = held[0, own, :].astype(f32) + other[0, own, :].astype(f32)
    for block in range(1, held.shape[0]):
        weights += held[block, own, :].astype(f32) + other[block, own, :].astype(f32)
    weights = weights.astype(bf16)
    for block in range(blocks):
        for part in range(width // lanes):
            piece = block * (width // lanes) + part
            payload[piece, :width, :] = acc[block, :, part * lanes : (part + 1) * lanes].astype(bf16)
            payload[piece, width:, :] = weights


def weights_kernel(terms, total):
    width = terms.shape[1] - total.shape[1]
    summed = terms[0, width:, :].astype(f32)
    for piece in range(1, terms.shape[0]):
        summed += terms[piece, width:, :].astype(f32)
    for piece in range(total.shape[0]):
        total[piece] = summed


def features_kernel(terms, w_msg, grad):
    width = w_msg.shape[0]
    summed = terms[0, :width, :].astype(f32)
    for piece in range(1, terms.shape[0]):
        summed += terms[piece, :width, :].astype(f32)
    grad[...] = lax.dot_general(
        summed.astype(bf16), w_msg[...], (((0,), (1,)), ((), ())), preferred_element_type=f32
    ).astype(bf16)


def in_vmem(count):
    return [pl.BlockSpec(memory_space=pltpu.VMEM)] * count


def in_smem(count):
    return [pl.BlockSpec(memory_space=pltpu.SMEM)] * count


def limits(mebibytes):
    return pltpu.CompilerParams(vmem_limit_bytes=mebibytes * 2**20)


def per_device(features, cotangent, w_msg, w_out, tile_vals, tile_emit, tile_recv, tile_count):
    own_rows = features[0]
    facet_rows, width = own_rows.shape
    tile_dim = tile_vals.shape[-1]
    emit_size = lax.axis_size("emit")
    recv_size = lax.axis_size("recv")
    recv_blocks = facet_rows * emit_size // tile_dim
    emit_blocks = facet_rows * recv_size // tile_dim
    chips = emit_size // 2
    lanes = width // 2
    values = tile_vals[0, 0]
    emit_slots = tile_emit[0, 0]
    recv_slots = tile_recv[0, 0]
    live = tile_count[0]
    core = lax.rem(lax.axis_index("emit"), 2)[None]
    same_core = [list(range(parity, emit_size, 2)) for parity in range(2)]
    swap = [(member, member ^ 1) for member in range(emit_size)]
    struct = jax.ShapeDtypeStruct
    in_hbm = pl.BlockSpec(memory_space=pltpu.HBM)

    group_rows = lax.all_to_all(
        jnp.broadcast_to(own_rows[None], (recv_size, facet_rows, width)), "recv", 0, 0, tiled=True
    )
    group_rows, emit_slots, recv_slots, live, core = lax.optimization_barrier(
        (group_rows, emit_slots, recv_slots, live, core)
    )
    kept, sent = pl.pallas_call(
        forward_kernel,
        out_shape=(
            struct((recv_blocks, tile_dim // 2, width), f32),
            struct((recv_blocks, tile_dim // 2, width), bf16),
        ),
        in_specs=in_smem(4) + in_vmem(1) + [in_hbm],
        out_specs=tuple(in_vmem(2)),
        scratch_shapes=[
            pltpu.VMEM((recv_blocks + 1, tile_dim, width), f32),
            pltpu.VMEM((ring_depth, group_tiles, tile_dim, tile_dim), bf16),
            pltpu.SemaphoreType.DMA((ring_depth,)),
        ],
        compiler_params=limits(48),
        name="forward_sweep",
    )(emit_slots, recv_slots, live, core, group_rows.reshape(emit_blocks, tile_dim, width), values)
    arrived = lax.ppermute(sent, "emit", swap)
    pair_sum = (kept + arrived.astype(f32)).astype(bf16)
    terms = lax.all_to_all(pair_sum, "emit", 0, 0, tiled=True, axis_index_groups=same_core)

    chunk = 4 * width // chips
    payload = pl.pallas_call(
        middle_kernel,
        out_shape=struct((chips, width + chunk, lanes), bf16),
        in_specs=in_vmem(4),
        out_specs=in_vmem(1)[0],
        compiler_params=limits(16),
        name="middle",
    )(terms, cotangent[0], w_msg, w_out)
    held = lax.all_to_all(payload, "emit", 0, 0, tiled=True, axis_index_groups=same_core)
    other = lax.ppermute(held, "emit", swap)

    back = pl.pallas_call(
        backward_kernel,
        out_shape=struct((recv_size, width + chunk // 2, lanes), bf16),
        in_specs=in_smem(4) + in_vmem(3),
        out_specs=in_vmem(1)[0],
        scratch_shapes=[
            pltpu.VMEM((recv_blocks, width, tile_dim), bf16),
            pltpu.VMEM((emit_blocks + 1, width, tile_dim), f32),
        ],
        compiler_params=limits(20),
        name="backward_sweep",
    )(recv_slots, emit_slots, live, core, held, other, values)
    back_terms = lax.all_to_all(back, "recv", 0, 0, tiled=True)

    total = pl.pallas_call(
        weights_kernel,
        out_shape=struct((emit_size, chunk // 2, lanes), f32),
        in_specs=in_vmem(1),
        out_specs=in_vmem(1)[0],
        compiler_params=limits(8),
        name="weights_sum",
    )(back_terms)
    gathered = lax.all_to_all(total, "emit", 0, 0, tiled=True).reshape(4, width, lanes)
    grad_features = pl.pallas_call(
        features_kernel,
        out_shape=struct((facet_rows, width), bf16),
        in_specs=in_vmem(2),
        out_specs=in_vmem(1)[0],
        compiler_params=limits(8),
        name="features_grad",
    )(back_terms, w_msg)[None]
    grad_w_out = jnp.concatenate([gathered[0], gathered[1]], axis=1)
    grad_w_msg = jnp.concatenate([gathered[2], gathered[3]], axis=1)
    return (grad_features, grad_w_msg, grad_w_out)


def solution(mesh):
    in_specs = (
        P("emit", "recv", None),
        P("recv", "emit", None),
        P(),
        P(),
        P("emit", "recv", None, None, None),
        P("emit", "recv", None),
        P("emit", "recv", None),
        P("emit", "recv"),
    )
    out_specs = (P("emit", "recv", None), P(), P())
    return jax.shard_map(
        per_device, mesh=mesh, in_specs=in_specs, out_specs=out_specs, check_vma=False
    )
```

```python
import functools

import jax
import jax.numpy as jnp
from jax import lax
from jax.experimental import pallas as pl
from jax.experimental.pallas import tpu as pltpu
from jax.sharding import PartitionSpec as P

ring_depth = 8
group_tiles = 8
f32 = jnp.float32
bf16 = jnp.bfloat16


def add_group(first, live, tiles, product, target, acc):
    spare = acc.shape[0] - 1
    slots = [first + at for at in range(group_tiles)]
    products = [product(slot, tiles[at]) for at, slot in enumerate(slots)]
    for slot, term in zip(slots, products):
        acc[jnp.where(slot < live, target[slot], spare)] += term


def sweep(live, tiles, ring, sems, prepare, product, target, acc):
    depth = ring.shape[0]
    steps = lax.div(live + group_tiles - 1, group_tiles)

    def copy(step):
        place = lax.rem(step, depth)
        return pltpu.make_async_copy(
            tiles.at[pl.ds(step * group_tiles, group_tiles)], ring.at[place], sems.at[place]
        )

    def begin(step, carry):
        copy(step).start()
        return carry

    lax.fori_loop(0, jnp.minimum(steps, depth), begin, 0)
    acc[...] = jnp.zeros_like(acc)
    prepare()

    def advance(step, carry):
        copy(step).wait()
        held = ring.at[lax.rem(step, depth)]
        add_group(step * group_tiles, live, held, product, target, acc)

        @pl.when(step + depth < steps)
        def _():
            copy(step + depth).start()

        return carry

    lax.fori_loop(0, steps, advance, 0)


def forward_kernel(
    source, target, live, place, own, pair, beside, across, tiles, kept, sent, rows, acc, ring, sems
):
    half = kept.shape[1]
    core, column, height = place[0], place[1], place[2]
    heights = rows.shape[0]

    def prepare():
        for held, base, side in (
            (own, height, column),
            (pair, height ^ 1, column),
            (beside, height, 1 - column),
            (across, height ^ 1, 1 - column),
        ):
            at = pl.ds(pl.multiple_of(side * half, half), half)
            for step in range(held.shape[0]):
                rows[lax.rem(base + heights - 2 * step, heights), at, :] = held[step]

    def product(slot, tile):
        return jnp.dot(tile, rows[source[slot]], preferred_element_type=f32)

    sweep(live[0], tiles, ring, sems, prepare, product, target, acc)
    mine = pl.multiple_of(core * half, half)
    other = pl.multiple_of((1 - core) * half, half)
    for block in range(kept.shape[0]):
        sent[block] = acc[block, pl.ds(other, half), :].astype(bf16)
        kept[block] = acc[block, pl.ds(mine, half), :]


def middle_kernel(terms, cotangent, w_msg, w_out, payload):
    width = w_msg.shape[0]
    pieces = terms.shape[0]
    lanes = width // 2
    summed = terms[0].astype(f32)
    for piece in range(1, pieces):
        summed += terms[piece].astype(f32)
    summed = summed.astype(bf16)
    message = jnp.dot(summed, w_msg[...], preferred_element_type=f32).astype(bf16)
    preact = jnp.dot(message, w_out[...], preferred_element_type=f32)
    sigmoid_pre = jax.nn.sigmoid(preact)
    slope = sigmoid_pre * (1.0 + preact * (1.0 - sigmoid_pre))
    grad_preact = (cotangent[...].astype(f32) * slope).astype(bf16)
    across = (((1,), (1,)), ((), ()))
    along = (((0,), (0,)), ((), ()))
    grad_turned = lax.dot_general(w_out[...], grad_preact, across, preferred_element_type=f32).astype(bf16)
    grad = lax.dot_general(grad_preact, w_out[...], across, preferred_element_type=f32).astype(bf16)
    out_part = lax.dot_general(message, grad_preact, along, preferred_element_type=f32).astype(bf16)
    msg_part = lax.dot_general(summed, grad, along, preferred_element_type=f32).astype(bf16)
    parts = (
        out_part[:, :lanes],
        out_part[:, lanes:],
        msg_part[:, :lanes],
        msg_part[:, lanes:],
    )
    chunk = 4 * width // pieces
    for piece in range(pieces):
        payload[piece, :width, :] = grad_turned
        at = 0
        while at < chunk:
            quarter, row = divmod(piece * chunk + at, width)
            size = min(chunk - at, width - row)
            payload[piece, width + at : width + at + size, :] = parts[quarter][row : row + size]
            at += size


def backward_kernel(
    source, target, live, place, held, other, tiles, own, pair, beside, across, grads, acc, ring, sems
):
    core, column, height = place[0], place[1], place[2]
    width, lanes = acc.shape[1], held.shape[2]
    heights = acc.shape[0] - 1
    chunk = (held.shape[1] - width) // 2

    def lay(first, second):
        for block in range(held.shape[0]):
            grads[block, :, :lanes] = first[block, :width, :]
            grads[block, :, lanes:] = second[block, :width, :]

    def prepare():
        @pl.when(core == 0)
        def _():
            lay(held, other)

        @pl.when(core == 1)
        def _():
            lay(other, held)

    def product(slot, tile):
        return jnp.dot(grads[source[slot]], tile, preferred_element_type=f32)

    sweep(live[0], tiles, ring, sems, prepare, product, target, acc)
    mine = pl.ds(pl.multiple_of(width + core * chunk, chunk), chunk)
    weights = held[0, mine, :].astype(f32) + other[0, mine, :].astype(f32)
    for block in range(1, held.shape[0]):
        weights += held[block, mine, :].astype(f32) + other[block, mine, :].astype(f32)
    weights = weights.astype(bf16)
    steps = heights // 2

    def hand_out(column):
        for out, base, side in (
            (own, height, column),
            (pair, height ^ 1, column),
            (beside, height, 1 - column),
            (across, height ^ 1, 1 - column),
        ):
            for step in range(steps):
                block = acc[lax.rem(base + 2 * step, heights), :, side * lanes : (side + 1) * lanes]
                out[step * width : (step + 1) * width, :] = block.astype(bf16)

    @pl.when(column == 0)
    def _():
        hand_out(0)

    @pl.when(column == 1)
    def _():
        hand_out(1)

    for out in (own, pair, beside, across):
        out[steps * width :, :] = weights


def quad_kernel(width, own, pair, beside, across, *outs):
    chunk = outs[0].shape[0] - width

    def total(at, size):
        rows = pl.ds(at, size)
        near = own[rows, :].astype(f32) + pair[rows, :].astype(f32)
        far = beside[rows, :].astype(f32) + across[rows, :].astype(f32)
        return (near + far).astype(bf16)

    weights = total(width * len(outs), chunk)
    for step, out in enumerate(outs):
        out[:width, :] = total(step * width, width)
        out[width:, :] = weights


def ring_sum(terms, rows):
    parts = [term[rows, :].astype(f32) for term in terms]
    while len(parts) > 1:
        half = len(parts) // 2
        parts = [near + far for near, far in zip(parts[:half], parts[half:])]
    return parts[0]


def weights_kernel(*refs):
    terms, total = refs[:-1], refs[-1]
    chunk = total.shape[1]
    summed = ring_sum(terms, pl.ds(terms[0].shape[0] - chunk, chunk))
    for piece in range(total.shape[0]):
        total[piece] = summed


def features_kernel(*refs):
    terms, w_msg, grad = refs[:-2], refs[-2], refs[-1]
    summed = ring_sum(terms, pl.ds(0, w_msg.shape[0]))
    grad[...] = lax.dot_general(
        summed.astype(bf16), w_msg[...], (((0,), (1,)), ((), ())), preferred_element_type=f32
    ).astype(bf16)


def in_vmem(count):
    return [pl.BlockSpec(memory_space=pltpu.VMEM)] * count


def in_smem(count):
    return [pl.BlockSpec(memory_space=pltpu.SMEM)] * count


def limits(mebibytes):
    return pltpu.CompilerParams(vmem_limit_bytes=mebibytes * 2**20)


def per_device(features, cotangent, w_msg, w_out, tile_vals, tile_emit, tile_recv, tile_count):
    own_rows = features[0]
    facet_rows, width = own_rows.shape
    tile_dim = tile_vals.shape[-1]
    emit_size = lax.axis_size("emit")
    recv_size = lax.axis_size("recv")
    recv_blocks = facet_rows * emit_size // tile_dim
    emit_blocks = facet_rows * recv_size // tile_dim
    chips = emit_size // 2
    lanes = width // 2
    values = tile_vals[0, 0]
    emit_slots = tile_emit[0, 0]
    recv_slots = tile_recv[0, 0]
    live = tile_count[0]
    heights = recv_size // 2
    steps = heights // 2
    recv_at = lax.axis_index("recv")
    place = jnp.stack([lax.rem(lax.axis_index("emit"), 2), lax.rem(recv_at, 2), lax.div(recv_at, 2)])
    same_core = [list(range(parity, emit_size, 2)) for parity in range(2)]
    swap = [(member, member ^ 1) for member in range(emit_size)]
    struct = jax.ShapeDtypeStruct
    in_hbm = pl.BlockSpec(memory_space=pltpu.HBM)
    sweep_scratch = [
        pltpu.VMEM((ring_depth, group_tiles, tile_dim, tile_dim), bf16),
        pltpu.SemaphoreType.DMA((ring_depth,)),
    ]

    def to_quad(array, bits):
        return lax.ppermute(array, "recv", [(member, member ^ bits) for member in range(recv_size)])

    def along_z(array, step):
        return lax.ppermute(
            array, "recv", [(member, (member + 4 * step) % recv_size) for member in range(recv_size)]
        )

    column_rows = jnp.stack([own_rows] + [along_z(own_rows, step) for step in range(1, steps)])
    kept, sent = pl.pallas_call(
        forward_kernel,
        out_shape=(
            struct((recv_blocks, tile_dim // 2, width), f32),
            struct((recv_blocks, tile_dim // 2, width), bf16),
        ),
        in_specs=in_smem(4) + in_vmem(4) + [in_hbm],
        out_specs=tuple(in_vmem(2)),
        scratch_shapes=[
            pltpu.VMEM((emit_blocks, tile_dim, width), bf16),
            pltpu.VMEM((recv_blocks + 1, tile_dim, width), f32),
        ]
        + sweep_scratch,
        compiler_params=limits(48),
        name="forward_sweep",
    )(
        emit_slots,
        recv_slots,
        live,
        place,
        column_rows,
        to_quad(column_rows, 2),
        to_quad(column_rows, 1),
        to_quad(column_rows, 3),
        values,
    )
    arrived = lax.ppermute(sent, "emit", swap)
    pair_sum = (kept + arrived.astype(f32)).astype(bf16)
    terms = lax.all_to_all(pair_sum, "emit", 0, 0, tiled=True, axis_index_groups=same_core)

    chunk = 4 * width // chips
    payload = pl.pallas_call(
        middle_kernel,
        out_shape=struct((chips, width + chunk, lanes), bf16),
        in_specs=in_vmem(4),
        out_specs=in_vmem(1)[0],
        compiler_params=limits(16),
        name="middle",
    )(terms, cotangent[0], w_msg, w_out)
    held = lax.all_to_all(payload, "emit", 0, 0, tiled=True, axis_index_groups=same_core)
    other = lax.ppermute(held, "emit", swap)

    spread = struct((steps * width + chunk // 2, lanes), bf16)
    own, pair, beside, across = pl.pallas_call(
        backward_kernel,
        out_shape=(spread,) * 4,
        in_specs=in_smem(4) + in_vmem(2) + [in_hbm],
        out_specs=tuple(in_vmem(4)),
        scratch_shapes=[
            pltpu.VMEM((recv_blocks, width, tile_dim), bf16),
            pltpu.VMEM((emit_blocks + 1, width, tile_dim), f32),
        ]
        + sweep_scratch,
        compiler_params=limits(48),
        name="backward_sweep",
    )(recv_slots, emit_slots, live, place, held, other, values)
    terms = pl.pallas_call(
        functools.partial(quad_kernel, width),
        out_shape=(struct((width + chunk // 2, lanes), bf16),) * steps,
        in_specs=in_vmem(4),
        out_specs=tuple(in_vmem(steps)),
        compiler_params=limits(8),
        name="quad_sum",
    )(own, to_quad(pair, 2), to_quad(beside, 1), to_quad(across, 3))
    terms = [terms[0]] + [along_z(terms[step], step) for step in range(1, steps)]

    total = pl.pallas_call(
        weights_kernel,
        out_shape=struct((emit_size, chunk // 2, lanes), f32),
        in_specs=in_vmem(steps),
        out_specs=in_vmem(1)[0],
        compiler_params=limits(8),
        name="weights_sum",
    )(*terms)
    gathered = lax.all_to_all(total, "emit", 0, 0, tiled=True).reshape(4, width, lanes)
    grad_features = pl.pallas_call(
        features_kernel,
        out_shape=struct((facet_rows, width), bf16),
        in_specs=in_vmem(steps + 1),
        out_specs=in_vmem(1)[0],
        compiler_params=limits(8),
        name="features_grad",
    )(*terms, w_msg)[None]
    grad_w_out = jnp.concatenate([gathered[0], gathered[1]], axis=1)
    grad_w_msg = jnp.concatenate([gathered[2], gathered[3]], axis=1)
    return (grad_features, grad_w_msg, grad_w_out)


def solution(mesh):
    in_specs = (
        P("emit", "recv", None),
        P("recv", "emit", None),
        P(),
        P(),
        P("emit", "recv", None, None, None),
        P("emit", "recv", None),
        P("emit", "recv", None),
        P("emit", "recv"),
    )
    out_specs = (P("emit", "recv", None), P(), P())
    return jax.shard_map(
        per_device, mesh=mesh, in_specs=in_specs, out_specs=out_specs, check_vma=False
    )
```

```python
import jax
import jax.numpy as jnp
from jax import lax
from jax.experimental import pallas as pl
from jax.experimental.pallas import tpu as pltpu
from jax.sharding import PartitionSpec as P

ring_depth = 8
group_tiles = 8
f32 = jnp.float32
bf16 = jnp.bfloat16


def add_group(first, live, tiles, product, target, acc):
    spare = acc.shape[0] - 1
    slots = [first + at for at in range(group_tiles)]
    products = [product(slot, tiles[at]) for at, slot in enumerate(slots)]
    for slot, term in zip(slots, products):
        acc[jnp.where(slot < live, target(slot), spare)] += term


def sweep(live, tiles, ring, sems, prepare, product, target, acc):
    depth = ring.shape[0]
    steps = lax.div(live + group_tiles - 1, group_tiles)

    def copy(step):
        place = lax.rem(step, depth)
        return pltpu.make_async_copy(
            tiles.at[pl.ds(step * group_tiles, group_tiles)], ring.at[place], sems.at[place]
        )

    def begin(step, carry):
        copy(step).start()
        return carry

    lax.fori_loop(0, jnp.minimum(steps, depth), begin, 0)
    acc[...] = jnp.zeros_like(acc)
    prepare()

    def advance(step, carry):
        copy(step).wait()
        held = ring.at[lax.rem(step, depth)]
        add_group(step * group_tiles, live, held, product, target, acc)

        @pl.when(step + depth < steps)
        def _():
            copy(step + depth).start()

        return carry

    lax.fori_loop(0, steps, advance, 0)


def unpack(numbers, slots):
    live, core, column, parity = (numbers[at] for at in range(4))
    return live, core, column, parity, lambda slot: numbers[4 + slot], lambda slot: numbers[4 + slots + slot]


def forward_kernel(
    numbers, own, pair, beside, across, tiles, kept, sent, rows, acc, ring, sems
):
    half = kept.shape[1]
    live, core, column, parity, emit_block, recv_block = unpack(numbers, tiles.shape[0])

    def prepare():
        for held, side, odd in (
            (own, column, parity),
            (pair, column, 1 - parity),
            (beside, 1 - column, parity),
            (across, 1 - column, 1 - parity),
        ):
            at = pl.ds(pl.multiple_of(side * half, half), half)
            for step in range(held.shape[0]):
                rows[2 * step + odd, at, :] = held[step]

    def product(slot, tile):
        return jnp.dot(tile, rows[emit_block(slot)], preferred_element_type=f32)

    sweep(live, tiles, ring, sems, prepare, product, recv_block, acc)
    mine = pl.multiple_of(core * half, half)
    other = pl.multiple_of((1 - core) * half, half)
    for block in range(kept.shape[0]):
        sent[block] = acc[block, pl.ds(other, half), :].astype(bf16)
        kept[block] = acc[block, pl.ds(mine, half), :]


def middle_kernel(terms, cotangent, w_msg, w_out, payload):
    width = w_msg.shape[0]
    pieces = terms.shape[0]
    lanes = width // 2
    summed = terms[0].astype(f32)
    for piece in range(1, pieces):
        summed += terms[piece].astype(f32)
    summed = summed.astype(bf16)
    message = jnp.dot(summed, w_msg[...], preferred_element_type=f32).astype(bf16)
    preact = jnp.dot(message, w_out[...], preferred_element_type=f32)
    sigmoid_pre = jax.nn.sigmoid(preact)
    slope = sigmoid_pre * (1.0 + preact * (1.0 - sigmoid_pre))
    grad_preact = (cotangent[...].astype(f32) * slope).astype(bf16)
    across = (((1,), (1,)), ((), ()))
    along = (((0,), (0,)), ((), ()))
    grad_turned = lax.dot_general(w_out[...], grad_preact, across, preferred_element_type=f32).astype(bf16)
    grad = lax.dot_general(grad_preact, w_out[...], across, preferred_element_type=f32).astype(bf16)
    out_part = lax.dot_general(message, grad_preact, along, preferred_element_type=f32).astype(bf16)
    msg_part = lax.dot_general(summed, grad, along, preferred_element_type=f32).astype(bf16)
    parts = (
        out_part[:, :lanes],
        out_part[:, lanes:],
        msg_part[:, :lanes],
        msg_part[:, lanes:],
    )
    chunk = 4 * width // pieces
    for piece in range(pieces):
        payload[piece, :width, :] = grad_turned
        at = 0
        while at < chunk:
            quarter, row = divmod(piece * chunk + at, width)
            size = min(chunk - at, width - row)
            payload[piece, width + at : width + at + size, :] = parts[quarter][row : row + size]
            at += size


def backward_kernel(
    numbers, held, other, tiles, own, pair, beside, across, grads, acc, ring, sems
):
    live, core, column, parity, emit_block, recv_block = unpack(numbers, tiles.shape[0])
    width, lanes = acc.shape[1], held.shape[2]
    chunk = (held.shape[1] - width) // 2
    steps = own.shape[0] // width

    def lay(first, second):
        for block in range(held.shape[0]):
            grads[block, :, :lanes] = first[block, :width, :]
            grads[block, :, lanes:] = second[block, :width, :]

    def prepare():
        @pl.when(core == 0)
        def _():
            lay(held, other)

        @pl.when(core == 1)
        def _():
            lay(other, held)

    def product(slot, tile):
        return jnp.dot(grads[recv_block(slot)], tile, preferred_element_type=f32)

    sweep(live, tiles, ring, sems, prepare, product, emit_block, acc)
    mine = pl.ds(pl.multiple_of(width + core * chunk, chunk), chunk)
    weights = held[0, mine, :].astype(f32) + other[0, mine, :].astype(f32)
    for block in range(1, held.shape[0]):
        weights += held[block, mine, :].astype(f32) + other[block, mine, :].astype(f32)
    weights = weights.astype(bf16)

    def hand_out(near):
        for out, side, odd in (
            (own, near, parity),
            (pair, near, 1 - parity),
            (beside, 1 - near, parity),
            (across, 1 - near, 1 - parity),
        ):
            for step in range(steps):
                block = acc[2 * step + odd, :, side * lanes : (side + 1) * lanes]
                out[step * width : (step + 1) * width, :] = block.astype(bf16)
            out[steps * width :, :] = weights

    @pl.when(column == 0)
    def _():
        hand_out(0)

    @pl.when(column == 1)
    def _():
        hand_out(1)


def quad_kernel(own, pair, beside, across, out):
    steps = out.shape[0]
    width = (own.shape[0] - out.shape[1]) // (steps - 1)

    def total(rows):
        near = own[rows, :].astype(f32) + pair[rows, :].astype(f32)
        far = beside[rows, :].astype(f32) + across[rows, :].astype(f32)
        return (near + far).astype(bf16)

    weights = total(slice(steps * width, None))
    for step in range(steps):
        out[step, :width, :] = total(slice(step * width, (step + 1) * width))
        out[step, width:, :] = weights


def step_sum(terms, rows):
    summed = terms[0, rows, :].astype(f32)
    for step in range(1, terms.shape[0]):
        summed += terms[step, rows, :].astype(f32)
    return summed


def weights_kernel(terms, total):
    chunk = total.shape[1]
    summed = step_sum(terms, pl.ds(terms.shape[1] - chunk, chunk))
    for piece in range(total.shape[0]):
        total[piece] = summed


def features_kernel(terms, w_msg, grad):
    grad[...] = lax.dot_general(
        step_sum(terms, pl.ds(0, w_msg.shape[0])).astype(bf16),
        w_msg[...],
        (((0,), (1,)), ((), ())),
        preferred_element_type=f32,
    ).astype(bf16)


def in_vmem(count):
    return [pl.BlockSpec(memory_space=pltpu.VMEM)] * count


def in_smem(count):
    return [pl.BlockSpec(memory_space=pltpu.SMEM)] * count


def limits(mebibytes):
    return pltpu.CompilerParams(vmem_limit_bytes=mebibytes * 2**20)


def per_device(features, cotangent, w_msg, w_out, tile_vals, tile_emit, tile_recv, tile_count):
    own_rows = features[0]
    facet_rows, width = own_rows.shape
    tile_dim = tile_vals.shape[-1]
    emit_size = lax.axis_size("emit")
    recv_size = lax.axis_size("recv")
    recv_blocks = facet_rows * emit_size // tile_dim
    emit_blocks = facet_rows * recv_size // tile_dim
    chips = emit_size // 2
    lanes = width // 2
    values = tile_vals[0, 0]
    steps = recv_size // 4
    recv_at = lax.axis_index("recv")
    column, parity = lax.rem(recv_at, 2), lax.rem(lax.div(recv_at, 2), 2)
    core = lax.rem(lax.axis_index("emit"), 2)
    numbers = jnp.concatenate(
        [tile_count[0], core[None], column[None], parity[None], tile_emit[0, 0], tile_recv[0, 0]]
    )
    same_core = [list(range(parity, emit_size, 2)) for parity in range(2)]
    swap = [(member, member ^ 1) for member in range(emit_size)]
    struct = jax.ShapeDtypeStruct
    in_hbm = pl.BlockSpec(memory_space=pltpu.HBM)
    sweep_scratch = [
        pltpu.VMEM((ring_depth, group_tiles, tile_dim, tile_dim), bf16),
        pltpu.SemaphoreType.DMA((ring_depth,)),
    ]

    def to_quad(array, bits):
        return lax.ppermute(array, "recv", [(member, member ^ bits) for member in range(recv_size)])

    def along_z(array):
        groups = [list(range(first, recv_size, 4)) for first in range(4)]
        return lax.all_to_all(array, "recv", 0, 0, tiled=True, axis_index_groups=groups)

    column_rows = along_z(jnp.broadcast_to(own_rows[None], (steps, facet_rows, width)))
    kept, sent = pl.pallas_call(
        forward_kernel,
        out_shape=(
            struct((recv_blocks, tile_dim // 2, width), f32),
            struct((recv_blocks, tile_dim // 2, width), bf16),
        ),
        in_specs=in_smem(1) + in_vmem(4) + [in_hbm],
        out_specs=tuple(in_vmem(2)),
        scratch_shapes=[
            pltpu.VMEM((emit_blocks, tile_dim, width), bf16),
            pltpu.VMEM((recv_blocks + 1, tile_dim, width), f32),
        ]
        + sweep_scratch,
        compiler_params=limits(48),
        name="forward_sweep",
    )(
        numbers,
        column_rows,
        to_quad(column_rows, 2),
        to_quad(column_rows, 1),
        to_quad(column_rows, 3),
        values,
    )
    arrived = lax.ppermute(sent, "emit", swap)
    pair_sum = (kept + arrived.astype(f32)).astype(bf16)
    terms = lax.all_to_all(pair_sum, "emit", 0, 0, tiled=True, axis_index_groups=same_core)

    chunk = 4 * width // chips
    payload = pl.pallas_call(
        middle_kernel,
        out_shape=struct((chips, width + chunk, lanes), bf16),
        in_specs=in_vmem(4),
        out_specs=in_vmem(1)[0],
        compiler_params=limits(16),
        name="middle",
    )(terms, cotangent[0], w_msg, w_out)
    held = lax.all_to_all(payload, "emit", 0, 0, tiled=True, axis_index_groups=same_core)
    other = lax.ppermute(held, "emit", swap)

    spread = struct((steps * width + chunk // 2, lanes), bf16)
    own, pair, beside, across = pl.pallas_call(
        backward_kernel,
        out_shape=(spread,) * 4,
        in_specs=in_smem(1) + in_vmem(2) + [in_hbm],
        out_specs=tuple(in_vmem(4)),
        scratch_shapes=[
            pltpu.VMEM((recv_blocks, width, tile_dim), bf16),
            pltpu.VMEM((emit_blocks + 1, width, tile_dim), f32),
        ]
        + sweep_scratch,
        compiler_params=limits(48),
        name="backward_sweep",
    )(numbers, held, other, values)
    terms = pl.pallas_call(
        quad_kernel,
        out_shape=struct((steps, width + chunk // 2, lanes), bf16),
        in_specs=in_vmem(4),
        out_specs=in_vmem(1)[0],
        compiler_params=limits(8),
        name="quad_sum",
    )(own, to_quad(pair, 2), to_quad(beside, 1), to_quad(across, 3))
    terms = along_z(terms)

    total = pl.pallas_call(
        weights_kernel,
        out_shape=struct((emit_size, chunk // 2, lanes), f32),
        in_specs=in_vmem(1),
        out_specs=in_vmem(1)[0],
        compiler_params=limits(8),
        name="weights_sum",
    )(terms)
    gathered = lax.all_to_all(total, "emit", 0, 0, tiled=True).reshape(4, width, lanes)
    grad_features = pl.pallas_call(
        features_kernel,
        out_shape=struct((facet_rows, width), bf16),
        in_specs=in_vmem(2),
        out_specs=in_vmem(1)[0],
        compiler_params=limits(8),
        name="features_grad",
    )(terms, w_msg)[None]
    grad_w_out = jnp.concatenate([gathered[0], gathered[1]], axis=1)
    grad_w_msg = jnp.concatenate([gathered[2], gathered[3]], axis=1)
    return (grad_features, grad_w_msg, grad_w_out)


def solution(mesh):
    in_specs = (
        P("emit", "recv", None),
        P("recv", "emit", None),
        P(),
        P(),
        P("emit", "recv", None, None, None),
        P("emit", "recv", None),
        P("emit", "recv", None),
        P("emit", "recv"),
    )
    out_specs = (P("emit", "recv", None), P(), P())
    return jax.shard_map(
        per_device, mesh=mesh, in_specs=in_specs, out_specs=out_specs, check_vma=False
    )
```

```python
import jax
import jax.numpy as jnp
from jax import lax
from jax.experimental import pallas as pl
from jax.experimental.pallas import tpu as pltpu
from jax.sharding import PartitionSpec as P

ring_depth = 8
group_tiles = 8
f32 = jnp.float32
bf16 = jnp.bfloat16


def add_group(first, live, tiles, product, target, acc):
    spare = acc.shape[0] - 1
    slots = [first + at for at in range(group_tiles)]
    products = [product(slot, tiles[at]) for at, slot in enumerate(slots)]
    for slot, term in zip(slots, products):
        acc[jnp.where(slot < live, target(slot), spare)] += term


def sweep(live, tiles, ring, sems, prepare, product, target, acc):
    depth = ring.shape[0]
    steps = lax.div(live + group_tiles - 1, group_tiles)

    def copy(step):
        place = lax.rem(step, depth)
        return pltpu.make_async_copy(
            tiles.at[pl.ds(step * group_tiles, group_tiles)], ring.at[place], sems.at[place]
        )

    def begin(step, carry):
        copy(step).start()
        return carry

    lax.fori_loop(0, jnp.minimum(steps, depth), begin, 0)
    acc[...] = jnp.zeros_like(acc)
    prepare()

    def advance(step, carry):
        copy(step).wait()
        held = ring.at[lax.rem(step, depth)]
        add_group(step * group_tiles, live, held, product, target, acc)

        @pl.when(step + depth < steps)
        def _():
            copy(step + depth).start()

        return carry

    lax.fori_loop(0, steps, advance, 0)


def unpack(numbers, slots):
    live, core, column, parity = (numbers[at] for at in range(4))
    return live, core, column, parity, lambda slot: numbers[5 + slot], lambda slot: numbers[5 + slots + slot]


def forward_kernel(
    numbers, own, pair, beside, across, tiles, kept, sent, rows, acc, ring, sems
):
    half = kept.shape[1]
    live, core, column, parity, emit_block, recv_block = unpack(numbers, tiles.shape[0])

    def prepare():
        for held, side, odd in (
            (own, column, parity),
            (pair, column, 1 - parity),
            (beside, 1 - column, parity),
            (across, 1 - column, 1 - parity),
        ):
            at = pl.ds(pl.multiple_of(side * half, half), half)
            for step in range(held.shape[0]):
                rows[2 * step + odd, at, :] = held[step]

    def product(slot, tile):
        return jnp.dot(tile, rows[emit_block(slot)], preferred_element_type=f32)

    sweep(live, tiles, ring, sems, prepare, product, recv_block, acc)
    mine = pl.multiple_of(core * half, half)
    other = pl.multiple_of((1 - core) * half, half)
    for block in range(kept.shape[0]):
        sent[block] = acc[block, pl.ds(other, half), :].astype(bf16)
        kept[block] = acc[block, pl.ds(mine, half), :]


def middle_kernel(terms, cotangent, w_msg, w_out, payload):
    width = w_msg.shape[0]
    pieces = terms.shape[0]
    lanes = width // 2
    summed = terms[0].astype(f32)
    for piece in range(1, pieces):
        summed += terms[piece].astype(f32)
    summed = summed.astype(bf16)
    message = jnp.dot(summed, w_msg[...], preferred_element_type=f32).astype(bf16)
    preact = jnp.dot(message, w_out[...], preferred_element_type=f32)
    sigmoid_pre = jax.nn.sigmoid(preact)
    slope = sigmoid_pre * (1.0 + preact * (1.0 - sigmoid_pre))
    grad_preact = (cotangent[...].astype(f32) * slope).astype(bf16)
    across = (((1,), (1,)), ((), ()))
    along = (((0,), (0,)), ((), ()))
    grad_turned = lax.dot_general(w_out[...], grad_preact, across, preferred_element_type=f32).astype(bf16)
    grad = lax.dot_general(grad_preact, w_out[...], across, preferred_element_type=f32).astype(bf16)
    out_part = lax.dot_general(message, grad_preact, along, preferred_element_type=f32).astype(bf16)
    msg_part = lax.dot_general(summed, grad, along, preferred_element_type=f32).astype(bf16)
    parts = (
        out_part[:, :lanes],
        out_part[:, lanes:],
        msg_part[:, :lanes],
        msg_part[:, lanes:],
    )
    chunk = 4 * width // pieces
    for piece in range(pieces):
        payload[piece, :width, :] = grad_turned
        at = 0
        while at < chunk:
            quarter, row = divmod(piece * chunk + at, width)
            size = min(chunk - at, width - row)
            payload[piece, width + at : width + at + size, :] = parts[quarter][row : row + size]
            at += size


def backward_kernel(
    numbers, held, other, tiles, own, pair, beside, across, grads, acc, ring, sems
):
    live, core, column, parity, emit_block, recv_block = unpack(numbers, tiles.shape[0])
    width, lanes = acc.shape[1], held.shape[2]
    steps = own.shape[0]

    def lay(first, second):
        for block in range(held.shape[0]):
            grads[block, :, :lanes] = first[block, :width, :]
            grads[block, :, lanes:] = second[block, :width, :]

    def prepare():
        @pl.when(core == 0)
        def _():
            lay(held, other)

        @pl.when(core == 1)
        def _():
            lay(other, held)

    def product(slot, tile):
        return jnp.dot(grads[recv_block(slot)], tile, preferred_element_type=f32)

    sweep(live, tiles, ring, sems, prepare, product, emit_block, acc)
    def hand_out(near):
        for out, side, odd in (
            (own, near, parity),
            (pair, near, 1 - parity),
            (beside, 1 - near, parity),
            (across, 1 - near, 1 - parity),
        ):
            for step in range(steps):
                block = acc[2 * step + odd, :, side * lanes : (side + 1) * lanes]
                out[step] = block.astype(bf16)

    @pl.when(column == 0)
    def _():
        hand_out(0)

    @pl.when(column == 1)
    def _():
        hand_out(1)


def chunk_kernel(numbers, held, other, out):
    chunk = out.shape[1]
    width = held.shape[1] - 2 * chunk
    mine = pl.ds(pl.multiple_of(width + numbers[1] * chunk, chunk), chunk)
    weights = held[0, mine, :].astype(f32) + other[0, mine, :].astype(f32)
    for block in range(1, held.shape[0]):
        weights += held[block, mine, :].astype(f32) + other[block, mine, :].astype(f32)
    for piece in range(out.shape[0]):
        out[piece] = weights.astype(bf16)


def quad_kernel(numbers, own, pair, beside, across, *outs):
    steps = own.shape[0]
    for step, out in enumerate(outs):
        block = lax.rem(numbers[4] + step, steps)
        near = own[block].astype(f32) + pair[block].astype(f32)
        far = beside[block].astype(f32) + across[block].astype(f32)
        out[...] = (near + far).astype(bf16)


def weights_kernel(terms, total):
    summed = terms[0].astype(f32)
    for piece in range(1, terms.shape[0]):
        summed += terms[piece].astype(f32)
    for piece in range(total.shape[0]):
        total[piece] = summed


def features_kernel(*refs):
    terms, w_msg, grad = refs[:-2], refs[-2], refs[-1]
    summed = terms[0][...].astype(f32)
    for term in terms[1:]:
        summed += term[...].astype(f32)
    grad[...] = lax.dot_general(
        summed.astype(bf16), w_msg[...], (((0,), (1,)), ((), ())), preferred_element_type=f32
    ).astype(bf16)


def in_vmem(count):
    return [pl.BlockSpec(memory_space=pltpu.VMEM)] * count


def in_smem(count):
    return [pl.BlockSpec(memory_space=pltpu.SMEM)] * count


def limits(mebibytes):
    return pltpu.CompilerParams(vmem_limit_bytes=mebibytes * 2**20)


def per_device(features, cotangent, w_msg, w_out, tile_vals, tile_emit, tile_recv, tile_count):
    own_rows = features[0]
    facet_rows, width = own_rows.shape
    tile_dim = tile_vals.shape[-1]
    emit_size = lax.axis_size("emit")
    recv_size = lax.axis_size("recv")
    recv_blocks = facet_rows * emit_size // tile_dim
    emit_blocks = facet_rows * recv_size // tile_dim
    chips = emit_size // 2
    lanes = width // 2
    values = tile_vals[0, 0]
    steps = recv_size // 4
    recv_at = lax.axis_index("recv")
    column, parity = lax.rem(recv_at, 2), lax.rem(lax.div(recv_at, 2), 2)
    core = lax.rem(lax.axis_index("emit"), 2)
    numbers = jnp.concatenate(
        [
            tile_count[0],
            jnp.stack([core, column, parity, lax.div(recv_at, 4)]),
            tile_emit[0, 0],
            tile_recv[0, 0],
        ]
    )
    same_core = [list(range(parity, emit_size, 2)) for parity in range(2)]
    swap = [(member, member ^ 1) for member in range(emit_size)]
    struct = jax.ShapeDtypeStruct
    in_hbm = pl.BlockSpec(memory_space=pltpu.HBM)
    sweep_scratch = [
        pltpu.VMEM((ring_depth, group_tiles, tile_dim, tile_dim), bf16),
        pltpu.SemaphoreType.DMA((ring_depth,)),
    ]

    sweep_cost = pl.CostEstimate(
        flops=2 * values.size * width, bytes_accessed=2 * values.size, transcendentals=0
    )

    def to_quad(array, bits):
        return lax.ppermute(array, "recv", [(member, member ^ bits) for member in range(recv_size)])

    def along_z(array, step):
        return lax.ppermute(
            array, "recv", [(member, (member + 4 * step) % recv_size) for member in range(recv_size)]
        )

    column_rows = lax.all_to_all(
        jnp.broadcast_to(own_rows[None], (steps, facet_rows, width)),
        "recv",
        0,
        0,
        tiled=True,
        axis_index_groups=[list(range(first, recv_size, 4)) for first in range(4)],
    )
    kept, sent = pl.pallas_call(
        forward_kernel,
        out_shape=(
            struct((recv_blocks, tile_dim // 2, width), f32),
            struct((recv_blocks, tile_dim // 2, width), bf16),
        ),
        in_specs=in_smem(1) + in_vmem(4) + [in_hbm],
        out_specs=tuple(in_vmem(2)),
        scratch_shapes=[
            pltpu.VMEM((emit_blocks, tile_dim, width), bf16),
            pltpu.VMEM((recv_blocks + 1, tile_dim, width), f32),
        ]
        + sweep_scratch,
        compiler_params=limits(48),
        cost_estimate=sweep_cost,
        name="forward_sweep",
    )(
        numbers,
        column_rows,
        to_quad(column_rows, 2),
        to_quad(column_rows, 1),
        to_quad(column_rows, 3),
        values,
    )
    arrived = lax.ppermute(sent, "emit", swap)
    pair_sum = (kept + arrived.astype(f32)).astype(bf16)
    terms = lax.all_to_all(pair_sum, "emit", 0, 0, tiled=True, axis_index_groups=same_core)

    chunk = 4 * width // chips
    payload = pl.pallas_call(
        middle_kernel,
        out_shape=struct((chips, width + chunk, lanes), bf16),
        in_specs=in_vmem(4),
        out_specs=in_vmem(1)[0],
        compiler_params=limits(16),
        name="middle",
    )(terms, cotangent[0], w_msg, w_out)
    held = lax.all_to_all(payload, "emit", 0, 0, tiled=True, axis_index_groups=same_core)
    other = lax.ppermute(held, "emit", swap)

    chunks = pl.pallas_call(
        chunk_kernel,
        out_shape=struct((recv_size, chunk // 2, lanes), bf16),
        in_specs=in_smem(1) + in_vmem(2),
        out_specs=in_vmem(1)[0],
        compiler_params=limits(8),
        name="weights_chunk",
    )(numbers, held, other)
    chunks = lax.all_to_all(chunks, "recv", 0, 0, tiled=True)

    own, pair, beside, across = pl.pallas_call(
        backward_kernel,
        out_shape=(struct((steps, width, lanes), bf16),) * 4,
        in_specs=in_smem(1) + in_vmem(2) + [in_hbm],
        out_specs=tuple(in_vmem(4)),
        scratch_shapes=[
            pltpu.VMEM((recv_blocks, width, tile_dim), bf16),
            pltpu.VMEM((emit_blocks + 1, width, tile_dim), f32),
        ]
        + sweep_scratch,
        compiler_params=limits(48),
        cost_estimate=sweep_cost,
        name="backward_sweep",
    )(numbers, held, other, values)
    terms = pl.pallas_call(
        quad_kernel,
        out_shape=(struct((width, lanes), bf16),) * steps,
        in_specs=in_smem(1) + in_vmem(4),
        out_specs=tuple(in_vmem(steps)),
        compiler_params=limits(8),
        name="quad_sum",
    )(numbers, own, to_quad(pair, 2), to_quad(beside, 1), to_quad(across, 3))
    chunks, terms = lax.optimization_barrier((chunks, terms))

    total = pl.pallas_call(
        weights_kernel,
        out_shape=struct((emit_size, chunk // 2, lanes), f32),
        in_specs=in_vmem(1),
        out_specs=in_vmem(1)[0],
        compiler_params=limits(8),
        name="weights_sum",
    )(chunks)
    gathered = lax.all_to_all(total, "emit", 0, 0, tiled=True).reshape(4, width, lanes)
    terms = [terms[0]] + [along_z(terms[step], step) for step in range(1, steps)]
    grad_features = pl.pallas_call(
        features_kernel,
        out_shape=struct((facet_rows, width), bf16),
        in_specs=in_vmem(steps + 1),
        out_specs=in_vmem(1)[0],
        compiler_params=limits(8),
        name="features_grad",
    )(*terms, w_msg)[None]
    grad_w_out = jnp.concatenate([gathered[0], gathered[1]], axis=1)
    grad_w_msg = jnp.concatenate([gathered[2], gathered[3]], axis=1)
    return (grad_features, grad_w_msg, grad_w_out)


def solution(mesh):
    in_specs = (
        P("emit", "recv", None),
        P("recv", "emit", None),
        P(),
        P(),
        P("emit", "recv", None, None, None),
        P("emit", "recv", None),
        P("emit", "recv", None),
        P("emit", "recv"),
    )
    out_specs = (P("emit", "recv", None), P(), P())
    return jax.shard_map(
        per_device, mesh=mesh, in_specs=in_specs, out_specs=out_specs, check_vma=False
    )
```

```python
import jax
import jax.numpy as jnp
from jax import lax
from jax.experimental import pallas as pl
from jax.experimental.pallas import tpu as pltpu
from jax.sharding import PartitionSpec as P

ring_depth = 8
group_tiles = 8
f32 = jnp.float32
bf16 = jnp.bfloat16


def add_group(first, live, tiles, product, target, acc):
    spare = acc.shape[0] - 1
    slots = [first + at for at in range(group_tiles)]
    products = [product(slot, tiles[at]) for at, slot in enumerate(slots)]
    for slot, term in zip(slots, products):
        acc[jnp.where(slot < live, target(slot), spare)] += term


def sweep(live, tiles, ring, sems, prepare, product, target, acc):
    depth = ring.shape[0]
    steps = lax.div(live + group_tiles - 1, group_tiles)

    def copy(step):
        place = lax.rem(step, depth)
        return pltpu.make_async_copy(
            tiles.at[pl.ds(step * group_tiles, group_tiles)], ring.at[place], sems.at[place]
        )

    def begin(step, carry):
        copy(step).start()
        return carry

    lax.fori_loop(0, jnp.minimum(steps, depth), begin, 0)
    acc[...] = jnp.zeros_like(acc)
    prepare()

    def advance(step, carry):
        copy(step).wait()
        held = ring.at[lax.rem(step, depth)]
        add_group(step * group_tiles, live, held, product, target, acc)

        @pl.when(step + depth < steps)
        def _():
            copy(step + depth).start()

        return carry

    lax.fori_loop(0, steps, advance, 0)


def unpack(numbers, slots):
    return *(numbers[at] for at in range(5)), lambda slot: numbers[5 + slot], lambda slot: numbers[5 + slots + slot]


def forward_kernel(
    numbers, own, pair, beside, across, tiles, kept, sent, rows, acc, ring, sems
):
    half = kept.shape[1]
    live, core, column, parity, height, emit_block, recv_block = unpack(numbers, tiles.shape[0])

    def prepare():
        for held, side, odd in (
            (own, column, parity),
            (pair, column, 1 - parity),
            (beside, 1 - column, parity),
            (across, 1 - column, 1 - parity),
        ):
            at = pl.ds(pl.multiple_of(side * half, half), half)
            steps = held.shape[0]
            for step in range(steps):
                rows[2 * lax.rem(height + steps - step, steps) + odd, at, :] = held[step]

    def product(slot, tile):
        return jnp.dot(tile, rows[emit_block(slot)], preferred_element_type=f32)

    sweep(live, tiles, ring, sems, prepare, product, recv_block, acc)
    mine = pl.multiple_of(core * half, half)
    other = pl.multiple_of((1 - core) * half, half)
    for block in range(kept.shape[0]):
        sent[block] = acc[block, pl.ds(other, half), :].astype(bf16)
        kept[block] = acc[block, pl.ds(mine, half), :]


def middle_kernel(terms, cotangent, w_msg, w_out, payload):
    width = w_msg.shape[0]
    pieces = terms.shape[0]
    lanes = width // 2
    summed = terms[0].astype(f32)
    for piece in range(1, pieces):
        summed += terms[piece].astype(f32)
    summed = summed.astype(bf16)
    message = jnp.dot(summed, w_msg[...], preferred_element_type=f32).astype(bf16)
    preact = jnp.dot(message, w_out[...], preferred_element_type=f32)
    sigmoid_pre = jax.nn.sigmoid(preact)
    slope = sigmoid_pre * (1.0 + preact * (1.0 - sigmoid_pre))
    grad_preact = (cotangent[...].astype(f32) * slope).astype(bf16)
    across = (((1,), (1,)), ((), ()))
    along = (((0,), (0,)), ((), ()))
    grad_turned = lax.dot_general(w_out[...], grad_preact, across, preferred_element_type=f32).astype(bf16)
    grad = lax.dot_general(grad_preact, w_out[...], across, preferred_element_type=f32).astype(bf16)
    out_part = lax.dot_general(message, grad_preact, along, preferred_element_type=f32).astype(bf16)
    msg_part = lax.dot_general(summed, grad, along, preferred_element_type=f32).astype(bf16)
    parts = (
        out_part[:, :lanes],
        out_part[:, lanes:],
        msg_part[:, :lanes],
        msg_part[:, lanes:],
    )
    chunk = 4 * width // pieces
    for piece in range(pieces):
        payload[piece, :width, :] = grad_turned
        at = 0
        while at < chunk:
            quarter, row = divmod(piece * chunk + at, width)
            size = min(chunk - at, width - row)
            payload[piece, width + at : width + at + size, :] = parts[quarter][row : row + size]
            at += size


def backward_kernel(
    numbers, held, other, tiles, own, pair, beside, across, weights, grads, acc, ring, sems
):
    live, core, column, parity, height, emit_block, recv_block = unpack(numbers, tiles.shape[0])
    width, lanes = acc.shape[1], held.shape[2]
    steps = own.shape[0]

    def lay(first, second):
        for block in range(held.shape[0]):
            grads[block, :, :lanes] = first[block, :width, :]
            grads[block, :, lanes:] = second[block, :width, :]

    def prepare():
        @pl.when(core == 0)
        def _():
            lay(held, other)

        @pl.when(core == 1)
        def _():
            lay(other, held)

    def product(slot, tile):
        return jnp.dot(grads[recv_block(slot)], tile, preferred_element_type=f32)

    sweep(live, tiles, ring, sems, prepare, product, emit_block, acc)
    chunk = weights.shape[1]
    mine = pl.ds(pl.multiple_of(width + core * chunk, chunk), chunk)
    summed = held[0, mine, :].astype(f32) + other[0, mine, :].astype(f32)
    for block in range(1, held.shape[0]):
        summed += held[block, mine, :].astype(f32) + other[block, mine, :].astype(f32)
    for piece in range(weights.shape[0]):
        weights[piece] = summed.astype(bf16)

    def hand_out(near):
        for out, side, odd in (
            (own, near, parity),
            (pair, near, 1 - parity),
            (beside, 1 - near, parity),
            (across, 1 - near, 1 - parity),
        ):
            for step in range(steps):
                at = 2 * lax.rem(height + step, steps) + odd
                block = acc[at, :, side * lanes : (side + 1) * lanes]
                out[step] = block.astype(bf16)

    @pl.when(column == 0)
    def _():
        hand_out(0)

    @pl.when(column == 1)
    def _():
        hand_out(1)


def quad_kernel(own, pair, beside, across, *outs):
    for step, out in enumerate(outs):
        near = own[step].astype(f32) + pair[step].astype(f32)
        far = beside[step].astype(f32) + across[step].astype(f32)
        out[...] = (near + far).astype(bf16)


def copy_kernel(source, out):
    out[...] = source[...]


def weights_kernel(terms, total):
    summed = terms[0].astype(f32)
    for piece in range(1, terms.shape[0]):
        summed += terms[piece].astype(f32)
    for piece in range(total.shape[0]):
        total[piece] = summed


def features_kernel(*refs):
    terms, w_msg, grad = refs[:-2], refs[-2], refs[-1]
    summed = terms[0][...].astype(f32)
    for term in terms[1:]:
        summed += term[...].astype(f32)
    grad[...] = lax.dot_general(
        summed.astype(bf16), w_msg[...], (((0,), (1,)), ((), ())), preferred_element_type=f32
    ).astype(bf16)


def in_vmem(count):
    return [pl.BlockSpec(memory_space=pltpu.VMEM)] * count


def in_smem(count):
    return [pl.BlockSpec(memory_space=pltpu.SMEM)] * count


def limits(mebibytes):
    return pltpu.CompilerParams(vmem_limit_bytes=mebibytes * 2**20)


def per_device(features, cotangent, w_msg, w_out, tile_vals, tile_emit, tile_recv, tile_count):
    own_rows = features[0]
    facet_rows, width = own_rows.shape
    tile_dim = tile_vals.shape[-1]
    emit_size = lax.axis_size("emit")
    recv_size = lax.axis_size("recv")
    recv_blocks = facet_rows * emit_size // tile_dim
    emit_blocks = facet_rows * recv_size // tile_dim
    chips = emit_size // 2
    lanes = width // 2
    values = tile_vals[0, 0]
    steps = recv_size // 4
    recv_at = lax.axis_index("recv")
    column, parity = lax.rem(recv_at, 2), lax.rem(lax.div(recv_at, 2), 2)
    core = lax.rem(lax.axis_index("emit"), 2)
    numbers = jnp.concatenate(
        [
            tile_count[0],
            jnp.stack([core, column, parity, lax.div(recv_at, 4)]),
            tile_emit[0, 0],
            tile_recv[0, 0],
        ]
    )
    same_core = [list(range(parity, emit_size, 2)) for parity in range(2)]
    swap = [(member, member ^ 1) for member in range(emit_size)]
    struct = jax.ShapeDtypeStruct
    in_hbm = pl.BlockSpec(memory_space=pltpu.HBM)
    sweep_scratch = [
        pltpu.VMEM((ring_depth, group_tiles, tile_dim, tile_dim), bf16),
        pltpu.SemaphoreType.DMA((ring_depth,)),
    ]

    sweep_cost = pl.CostEstimate(
        flops=2 * values.size * width, bytes_accessed=2 * values.size, transcendentals=0
    )

    def to_quad(array, bits):
        return lax.ppermute(array, "recv", [(member, member ^ bits) for member in range(recv_size)])

    def along_z(array, step):
        return lax.ppermute(
            array, "recv", [(member, (member + 4 * step) % recv_size) for member in range(recv_size)]
        )

    arrivals = {step: along_z(own_rows, step) for step in sorted(range(1, steps), key=lambda step: abs(2 * step - steps))}
    held_rows = pl.pallas_call(
        copy_kernel,
        out_shape=struct(own_rows.shape, bf16),
        in_specs=in_vmem(1),
        out_specs=in_vmem(1)[0],
        compiler_params=limits(8),
        name="own_rows",
    )(own_rows)
    column_rows = jnp.stack([held_rows] + [arrivals[step] for step in range(1, steps)])
    kept, sent = pl.pallas_call(
        forward_kernel,
        out_shape=(
            struct((recv_blocks, tile_dim // 2, width), f32),
            struct((recv_blocks, tile_dim // 2, width), bf16),
        ),
        in_specs=in_smem(1) + in_vmem(4) + [in_hbm],
        out_specs=tuple(in_vmem(2)),
        scratch_shapes=[
            pltpu.VMEM((emit_blocks, tile_dim, width), bf16),
            pltpu.VMEM((recv_blocks + 1, tile_dim, width), f32),
        ]
        + sweep_scratch,
        compiler_params=limits(48),
        cost_estimate=sweep_cost,
        name="forward_sweep",
    )(
        numbers,
        column_rows,
        to_quad(column_rows, 2),
        to_quad(column_rows, 1),
        to_quad(column_rows, 3),
        values,
    )
    arrived = lax.ppermute(sent, "emit", swap)
    pair_sum = (kept + arrived.astype(f32)).astype(bf16)
    terms = lax.all_to_all(pair_sum, "emit", 0, 0, tiled=True, axis_index_groups=same_core)

    chunk = 4 * width // chips
    payload = pl.pallas_call(
        middle_kernel,
        out_shape=struct((chips, width + chunk, lanes), bf16),
        in_specs=in_vmem(4),
        out_specs=in_vmem(1)[0],
        compiler_params=limits(16),
        name="middle",
    )(terms, cotangent[0], w_msg, w_out)
    held = lax.all_to_all(payload, "emit", 0, 0, tiled=True, axis_index_groups=same_core)
    other = lax.ppermute(held, "emit", swap)

    own, pair, beside, across, weights = pl.pallas_call(
        backward_kernel,
        out_shape=(struct((steps, width, lanes), bf16),) * 4
        + (struct((recv_size, chunk // 2, lanes), bf16),),
        in_specs=in_smem(1) + in_vmem(2) + [in_hbm],
        out_specs=tuple(in_vmem(5)),
        scratch_shapes=[
            pltpu.VMEM((recv_blocks, width, tile_dim), bf16),
            pltpu.VMEM((emit_blocks + 1, width, tile_dim), f32),
        ]
        + sweep_scratch,
        compiler_params=limits(48),
        cost_estimate=sweep_cost,
        name="backward_sweep",
    )(numbers, held, other, values)
    pair, weights = lax.optimization_barrier((to_quad(pair, 2), weights))
    chunks = lax.all_to_all(weights, "recv", 0, 0, tiled=True)
    terms = pl.pallas_call(
        quad_kernel,
        out_shape=(struct((width, lanes), bf16),) * steps,
        in_specs=in_vmem(4),
        out_specs=tuple(in_vmem(steps)),
        compiler_params=limits(8),
        name="quad_sum",
    )(own, pair, to_quad(beside, 1), to_quad(across, 3))
    terms = [terms[0]] + [along_z(terms[step], step) for step in range(1, steps)]
    chunks, terms[1] = lax.optimization_barrier((chunks, terms[1]))

    total = pl.pallas_call(
        weights_kernel,
        out_shape=struct((emit_size, chunk // 2, lanes), f32),
        in_specs=in_vmem(1),
        out_specs=in_vmem(1)[0],
        compiler_params=limits(8),
        name="weights_sum",
    )(chunks)
    gathered = lax.all_to_all(total, "emit", 0, 0, tiled=True).reshape(4, width, lanes)
    grad_features = pl.pallas_call(
        features_kernel,
        out_shape=struct((facet_rows, width), bf16),
        in_specs=in_vmem(steps + 1),
        out_specs=in_vmem(1)[0],
        compiler_params=limits(8),
        name="features_grad",
    )(*terms, w_msg)[None]
    grad_w_out = jnp.concatenate([gathered[0], gathered[1]], axis=1)
    grad_w_msg = jnp.concatenate([gathered[2], gathered[3]], axis=1)
    return (grad_features, grad_w_msg, grad_w_out)


def solution(mesh):
    in_specs = (
        P("emit", "recv", None),
        P("recv", "emit", None),
        P(),
        P(),
        P("emit", "recv", None, None, None),
        P("emit", "recv", None),
        P("emit", "recv", None),
        P("emit", "recv"),
    )
    out_specs = (P("emit", "recv", None), P(), P())
    return jax.shard_map(
        per_device, mesh=mesh, in_specs=in_specs, out_specs=out_specs, check_vma=False
    )
```

```python
import jax
import jax.numpy as jnp
from jax import lax
from jax.experimental import pallas as pl
from jax.experimental.pallas import tpu as pltpu
from jax.sharding import PartitionSpec as P

ring_depth = 8
group_tiles = 8
f32 = jnp.float32
bf16 = jnp.bfloat16


def add_group(first, live, tiles, product, target, acc):
    spare = acc.shape[0] - 1
    slots = [first + at for at in range(group_tiles)]
    products = [product(slot, tiles[at]) for at, slot in enumerate(slots)]
    for slot, term in zip(slots, products):
        acc[jnp.where(slot < live, target(slot), spare)] += term


def sweep(live, tiles, ring, sems, prepare, product, target, acc):
    depth = ring.shape[0]
    steps = lax.div(live + group_tiles - 1, group_tiles)

    def copy(step):
        place = lax.rem(step, depth)
        return pltpu.make_async_copy(
            tiles.at[pl.ds(step * group_tiles, group_tiles)], ring.at[place], sems.at[place]
        )

    def begin(step, carry):
        copy(step).start()
        return carry

    lax.fori_loop(0, jnp.minimum(steps, depth), begin, 0)
    acc[...] = jnp.zeros_like(acc)
    prepare()

    def advance(step, carry):
        copy(step).wait()
        held = ring.at[lax.rem(step, depth)]
        add_group(step * group_tiles, live, held, product, target, acc)

        @pl.when(step + depth < steps)
        def _():
            copy(step + depth).start()

        return carry

    lax.fori_loop(0, steps, advance, 0)


def unpack(numbers, slots):
    return *(numbers[at] for at in range(5)), lambda slot: numbers[5 + slot], lambda slot: numbers[5 + slots + slot]


def forward_kernel(
    numbers, own, pair, beside, across, tiles, kept, sent, rows, acc, ring, sems
):
    half = kept.shape[1]
    live, core, column, parity, height, emit_block, recv_block = unpack(numbers, tiles.shape[0])

    def prepare():
        for held, side, odd in (
            (own, column, parity),
            (pair, column, 1 - parity),
            (beside, 1 - column, parity),
            (across, 1 - column, 1 - parity),
        ):
            at = pl.ds(pl.multiple_of(side * half, half), half)
            steps = held.shape[0]
            for step in range(steps):
                rows[2 * lax.rem(height + steps - step, steps) + odd, at, :] = held[step]

    def product(slot, tile):
        return jnp.dot(tile, rows[emit_block(slot)], preferred_element_type=f32)

    sweep(live, tiles, ring, sems, prepare, product, recv_block, acc)
    mine = pl.multiple_of(core * half, half)
    other = pl.multiple_of((1 - core) * half, half)
    for block in range(kept.shape[0]):
        sent[block] = acc[block, pl.ds(other, half), :].astype(bf16)
        kept[block] = acc[block, pl.ds(mine, half), :]


def middle_kernel(terms, cotangent, w_msg, w_out, payload):
    width = w_msg.shape[0]
    pieces = terms.shape[0]
    lanes = width // 2
    summed = terms[0].astype(f32)
    for piece in range(1, pieces):
        summed += terms[piece].astype(f32)
    summed = summed.astype(bf16)
    message = jnp.dot(summed, w_msg[...], preferred_element_type=f32).astype(bf16)
    preact = jnp.dot(message, w_out[...], preferred_element_type=f32)
    sigmoid_pre = jax.nn.sigmoid(preact)
    slope = sigmoid_pre * (1.0 + preact * (1.0 - sigmoid_pre))
    grad_preact = (cotangent[...].astype(f32) * slope).astype(bf16)
    across = (((1,), (1,)), ((), ()))
    along = (((0,), (0,)), ((), ()))
    grad_turned = lax.dot_general(w_out[...], grad_preact, across, preferred_element_type=f32).astype(bf16)
    grad = lax.dot_general(grad_preact, w_out[...], across, preferred_element_type=f32).astype(bf16)
    out_part = lax.dot_general(message, grad_preact, along, preferred_element_type=f32).astype(bf16)
    msg_part = lax.dot_general(summed, grad, along, preferred_element_type=f32).astype(bf16)
    parts = (
        out_part[:, :lanes],
        out_part[:, lanes:],
        msg_part[:, :lanes],
        msg_part[:, lanes:],
    )
    chunk = 4 * width // pieces
    for piece in range(pieces):
        payload[piece, :width, :] = grad_turned
        at = 0
        while at < chunk:
            quarter, row = divmod(piece * chunk + at, width)
            size = min(chunk - at, width - row)
            payload[piece, width + at : width + at + size, :] = parts[quarter][row : row + size]
            at += size


def backward_kernel(
    numbers, held, other, tiles, own, pair, beside, across, weights, grads, acc, ring, sems
):
    live, core, column, parity, height, emit_block, recv_block = unpack(numbers, tiles.shape[0])
    width, lanes = acc.shape[1], held.shape[2]
    steps = own.shape[0]

    def lay(first, second):
        for block in range(held.shape[0]):
            grads[block, :, :lanes] = first[block, :width, :]
            grads[block, :, lanes:] = second[block, :width, :]

    def prepare():
        @pl.when(core == 0)
        def _():
            lay(held, other)

        @pl.when(core == 1)
        def _():
            lay(other, held)

    def product(slot, tile):
        return jnp.dot(grads[recv_block(slot)], tile, preferred_element_type=f32)

    sweep(live, tiles, ring, sems, prepare, product, emit_block, acc)
    chunk = weights.shape[1]
    mine = pl.ds(pl.multiple_of(width + core * chunk, chunk), chunk)
    summed = held[0, mine, :].astype(f32) + other[0, mine, :].astype(f32)
    for block in range(1, held.shape[0]):
        summed += held[block, mine, :].astype(f32) + other[block, mine, :].astype(f32)
    for piece in range(weights.shape[0]):
        weights[piece] = summed.astype(bf16)

    def hand_out(near):
        for out, side, odd in (
            (own, near, parity),
            (pair, near, 1 - parity),
            (beside, 1 - near, parity),
            (across, 1 - near, 1 - parity),
        ):
            for step in range(steps):
                at = 2 * lax.rem(height + step, steps) + odd
                block = acc[at, :, side * lanes : (side + 1) * lanes]
                out[step] = block.astype(bf16)

    @pl.when(column == 0)
    def _():
        hand_out(0)

    @pl.when(column == 1)
    def _():
        hand_out(1)


def quad_kernel(own, pair, beside, across, *outs):
    for step, out in enumerate(outs):
        near = own[step].astype(f32) + pair[step].astype(f32)
        far = beside[step].astype(f32) + across[step].astype(f32)
        out[...] = (near + far).astype(bf16)


def weights_kernel(terms, total):
    summed = terms[0].astype(f32)
    for piece in range(1, terms.shape[0]):
        summed += terms[piece].astype(f32)
    for piece in range(total.shape[0]):
        total[piece] = summed


def features_kernel(*refs):
    terms, w_msg, grad = refs[:-2], refs[-2], refs[-1]
    summed = terms[0][...].astype(f32)
    for term in terms[1:]:
        summed += term[...].astype(f32)
    grad[...] = lax.dot_general(
        summed.astype(bf16), w_msg[...], (((0,), (1,)), ((), ())), preferred_element_type=f32
    ).astype(bf16)


def in_vmem(count):
    return [pl.BlockSpec(memory_space=pltpu.VMEM)] * count


def in_smem(count):
    return [pl.BlockSpec(memory_space=pltpu.SMEM)] * count


def limits(mebibytes):
    return pltpu.CompilerParams(vmem_limit_bytes=mebibytes * 2**20)


def per_device(features, cotangent, w_msg, w_out, tile_vals, tile_emit, tile_recv, tile_count):
    own_rows = features[0]
    facet_rows, width = own_rows.shape
    tile_dim = tile_vals.shape[-1]
    emit_size = lax.axis_size("emit")
    recv_size = lax.axis_size("recv")
    recv_blocks = facet_rows * emit_size // tile_dim
    emit_blocks = facet_rows * recv_size // tile_dim
    chips = emit_size // 2
    lanes = width // 2
    values = tile_vals[0, 0]
    steps = recv_size // 4
    recv_at = lax.axis_index("recv")
    column, parity = lax.rem(recv_at, 2), lax.rem(lax.div(recv_at, 2), 2)
    core = lax.rem(lax.axis_index("emit"), 2)
    numbers = jnp.concatenate(
        [
            tile_count[0],
            jnp.stack([core, column, parity, lax.div(recv_at, 4)]),
            tile_emit[0, 0],
            tile_recv[0, 0],
        ]
    )
    same_core = [list(range(parity, emit_size, 2)) for parity in range(2)]
    swap = [(member, member ^ 1) for member in range(emit_size)]
    struct = jax.ShapeDtypeStruct
    in_hbm = pl.BlockSpec(memory_space=pltpu.HBM)
    sweep_scratch = [
        pltpu.VMEM((ring_depth, group_tiles, tile_dim, tile_dim), bf16),
        pltpu.SemaphoreType.DMA((ring_depth,)),
    ]

    sweep_cost = pl.CostEstimate(
        flops=2 * values.size * width, bytes_accessed=2 * values.size, transcendentals=0
    )

    def to_quad(array, bits):
        return lax.ppermute(array, "recv", [(member, member ^ bits) for member in range(recv_size)])

    def along_z(array, step):
        return lax.ppermute(
            array, "recv", [(member, (member + 4 * step) % recv_size) for member in range(recv_size)]
        )

    arrivals = {step: along_z(own_rows, step) for step in sorted(range(1, steps), key=lambda step: abs(2 * step - steps))}
    column_rows = jnp.stack([own_rows] + [arrivals[step] for step in range(1, steps)])
    kept, sent = pl.pallas_call(
        forward_kernel,
        out_shape=(
            struct((recv_blocks, tile_dim // 2, width), f32),
            struct((recv_blocks, tile_dim // 2, width), bf16),
        ),
        in_specs=in_smem(1) + in_vmem(4) + [in_hbm],
        out_specs=tuple(in_vmem(2)),
        scratch_shapes=[
            pltpu.VMEM((emit_blocks, tile_dim, width), bf16),
            pltpu.VMEM((recv_blocks + 1, tile_dim, width), f32),
        ]
        + sweep_scratch,
        compiler_params=limits(48),
        cost_estimate=sweep_cost,
        name="forward_sweep",
    )(
        numbers,
        column_rows,
        to_quad(column_rows, 2),
        to_quad(column_rows, 1),
        to_quad(column_rows, 3),
        values,
    )
    arrived = lax.ppermute(sent, "emit", swap)
    pair_sum = (kept + arrived.astype(f32)).astype(bf16)
    terms = lax.all_to_all(pair_sum, "emit", 0, 0, tiled=True, axis_index_groups=same_core)

    chunk = 4 * width // chips
    payload = pl.pallas_call(
        middle_kernel,
        out_shape=struct((chips, width + chunk, lanes), bf16),
        in_specs=in_vmem(4),
        out_specs=in_vmem(1)[0],
        compiler_params=limits(16),
        name="middle",
    )(terms, cotangent[0], w_msg, w_out)
    held = lax.all_to_all(payload, "emit", 0, 0, tiled=True, axis_index_groups=same_core)
    other = lax.ppermute(held, "emit", swap)

    own, pair, beside, across, weights = pl.pallas_call(
        backward_kernel,
        out_shape=(struct((steps, width, lanes), bf16),) * 4
        + (struct((recv_size, chunk // 2, lanes), bf16),),
        in_specs=in_smem(1) + in_vmem(2) + [in_hbm],
        out_specs=tuple(in_vmem(5)),
        scratch_shapes=[
            pltpu.VMEM((recv_blocks, width, tile_dim), bf16),
            pltpu.VMEM((emit_blocks + 1, width, tile_dim), f32),
        ]
        + sweep_scratch,
        compiler_params=limits(48),
        cost_estimate=sweep_cost,
        name="backward_sweep",
    )(numbers, held, other, values)
    chunks = lax.all_to_all(weights, "recv", 0, 0, tiled=True)
    terms = pl.pallas_call(
        quad_kernel,
        out_shape=(struct((width, lanes), bf16),) * steps,
        in_specs=in_vmem(4),
        out_specs=tuple(in_vmem(steps)),
        compiler_params=limits(8),
        name="quad_sum",
    )(own, to_quad(pair, 2), to_quad(beside, 1), to_quad(across, 3))
    chunks, terms = lax.optimization_barrier((chunks, terms))

    total = pl.pallas_call(
        weights_kernel,
        out_shape=struct((emit_size, chunk // 2, lanes), f32),
        in_specs=in_vmem(1),
        out_specs=in_vmem(1)[0],
        compiler_params=limits(8),
        name="weights_sum",
    )(chunks)
    gathered = lax.all_to_all(total, "emit", 0, 0, tiled=True).reshape(4, width, lanes)
    terms = [terms[0]] + [along_z(terms[step], step) for step in range(1, steps)]
    grad_features = pl.pallas_call(
        features_kernel,
        out_shape=struct((facet_rows, width), bf16),
        in_specs=in_vmem(steps + 1),
        out_specs=in_vmem(1)[0],
        compiler_params=limits(8),
        name="features_grad",
    )(*terms, w_msg)[None]
    grad_w_out = jnp.concatenate([gathered[0], gathered[1]], axis=1)
    grad_w_msg = jnp.concatenate([gathered[2], gathered[3]], axis=1)
    return (grad_features, grad_w_msg, grad_w_out)


def solution(mesh):
    in_specs = (
        P("emit", "recv", None),
        P("recv", "emit", None),
        P(),
        P(),
        P("emit", "recv", None, None, None),
        P("emit", "recv", None),
        P("emit", "recv", None),
        P("emit", "recv"),
    )
    out_specs = (P("emit", "recv", None), P(), P())
    return jax.shard_map(
        per_device, mesh=mesh, in_specs=in_specs, out_specs=out_specs, check_vma=False
    )
```

```python
import jax
import jax.numpy as jnp
from jax import lax
from jax.experimental import pallas as pl
from jax.experimental.pallas import tpu as pltpu
from jax.sharding import PartitionSpec as P

ring_depth = 8
group_tiles = 8
f32 = jnp.float32
bf16 = jnp.bfloat16


def add_group(first, live, tiles, product, target, acc):
    spare = acc.shape[0] - 1
    slots = [first + at for at in range(group_tiles)]
    products = [product(slot, tiles[at]) for at, slot in enumerate(slots)]
    for slot, term in zip(slots, products):
        acc[jnp.where(slot < live, target(slot), spare)] += term


def sweep(live, tiles, ring, sems, prepare, product, target, acc):
    depth = ring.shape[0]
    steps = lax.div(live + group_tiles - 1, group_tiles)

    def copy(step):
        place = lax.rem(step, depth)
        return pltpu.make_async_copy(
            tiles.at[pl.ds(step * group_tiles, group_tiles)], ring.at[place], sems.at[place]
        )

    def begin(step, carry):
        copy(step).start()
        return carry

    lax.fori_loop(0, jnp.minimum(steps, depth), begin, 0)
    acc[...] = jnp.zeros_like(acc)
    prepare()

    def advance(step, carry):
        copy(step).wait()
        held = ring.at[lax.rem(step, depth)]
        add_group(step * group_tiles, live, held, product, target, acc)

        @pl.when(step + depth < steps)
        def _():
            copy(step + depth).start()

        return carry

    lax.fori_loop(0, steps, advance, 0)


def unpack(numbers, slots):
    return *(numbers[at] for at in range(5)), lambda slot: numbers[5 + slot], lambda slot: numbers[5 + slots + slot]


def forward_kernel(
    numbers, own, pair, beside, across, tiles, kept, sent, rows, acc, ring, sems
):
    half = kept.shape[1]
    live, core, column, parity, height, emit_block, recv_block = unpack(numbers, tiles.shape[0])

    def prepare():
        for held, side, odd in (
            (own, column, parity),
            (pair, column, 1 - parity),
            (beside, 1 - column, parity),
            (across, 1 - column, 1 - parity),
        ):
            at = pl.ds(pl.multiple_of(side * half, half), half)
            steps = held.shape[0]
            for step in range(steps):
                rows[2 * lax.rem(height + steps - step, steps) + odd, at, :] = held[step]

    def product(slot, tile):
        return jnp.dot(tile, rows[emit_block(slot)], preferred_element_type=f32)

    sweep(live, tiles, ring, sems, prepare, product, recv_block, acc)
    mine = pl.multiple_of(core * half, half)
    other = pl.multiple_of((1 - core) * half, half)
    for block in range(kept.shape[0]):
        sent[block] = acc[block, pl.ds(other, half), :].astype(bf16)
        kept[block] = acc[block, pl.ds(mine, half), :]


def middle_kernel(terms, cotangent, w_msg, w_out, payload):
    width = w_msg.shape[0]
    pieces = terms.shape[0]
    lanes = width // 2
    summed = terms[0].astype(f32)
    for piece in range(1, pieces):
        summed += terms[piece].astype(f32)
    summed = summed.astype(bf16)
    message = jnp.dot(summed, w_msg[...], preferred_element_type=f32).astype(bf16)
    preact = jnp.dot(message, w_out[...], preferred_element_type=f32)
    sigmoid_pre = jax.nn.sigmoid(preact)
    slope = sigmoid_pre * (1.0 + preact * (1.0 - sigmoid_pre))
    grad_preact = (cotangent[...].astype(f32) * slope).astype(bf16)
    across = (((1,), (1,)), ((), ()))
    along = (((0,), (0,)), ((), ()))
    grad_turned = lax.dot_general(w_out[...], grad_preact, across, preferred_element_type=f32).astype(bf16)
    grad = lax.dot_general(grad_preact, w_out[...], across, preferred_element_type=f32).astype(bf16)
    out_part = lax.dot_general(message, grad_preact, along, preferred_element_type=f32).astype(bf16)
    msg_part = lax.dot_general(summed, grad, along, preferred_element_type=f32).astype(bf16)
    parts = (
        out_part[:, :lanes],
        out_part[:, lanes:],
        msg_part[:, :lanes],
        msg_part[:, lanes:],
    )
    chunk = 4 * width // pieces
    for piece in range(pieces):
        payload[piece, :width, :] = grad_turned
        at = 0
        while at < chunk:
            quarter, row = divmod(piece * chunk + at, width)
            size = min(chunk - at, width - row)
            payload[piece, width + at : width + at + size, :] = parts[quarter][row : row + size]
            at += size


def backward_kernel(
    numbers, held, other, tiles, own, pair, beside, across, grads, acc, ring, sems
):
    live, core, column, parity, height, emit_block, recv_block = unpack(numbers, tiles.shape[0])
    width, lanes = acc.shape[1], held.shape[2]
    steps = own.shape[0]

    def lay(first, second):
        for block in range(held.shape[0]):
            grads[block, :, :lanes] = first[block, :width, :]
            grads[block, :, lanes:] = second[block, :width, :]

    def prepare():
        @pl.when(core == 0)
        def _():
            lay(held, other)

        @pl.when(core == 1)
        def _():
            lay(other, held)

    def product(slot, tile):
        return jnp.dot(grads[recv_block(slot)], tile, preferred_element_type=f32)

    sweep(live, tiles, ring, sems, prepare, product, emit_block, acc)
    def hand_out(near):
        for out, side, odd in (
            (own, near, parity),
            (pair, near, 1 - parity),
            (beside, 1 - near, parity),
            (across, 1 - near, 1 - parity),
        ):
            for step in range(steps):
                at = 2 * lax.rem(height + step, steps) + odd
                block = acc[at, :, side * lanes : (side + 1) * lanes]
                out[step] = block.astype(bf16)

    @pl.when(column == 0)
    def _():
        hand_out(0)

    @pl.when(column == 1)
    def _():
        hand_out(1)


def copy_kernel(source, out):
    out[...] = source[...]


def chunk_kernel(held, other, second_core, out):
    chunk = out.shape[1]
    width = held.shape[1] - 2 * chunk

    def summed(rows):
        total = held[0, rows, :].astype(f32) + other[0, rows, :].astype(f32)
        for block in range(1, held.shape[0]):
            total += held[block, rows, :].astype(f32) + other[block, rows, :].astype(f32)
        return total

    first, second = summed(slice(width, width + chunk)), summed(slice(width + chunk, None))
    mine = jnp.where(second_core[0:1, :] > 0.5, second, first).astype(bf16)
    for piece in range(out.shape[0]):
        out[piece] = mine


def quad_kernel(own, pair, beside, across, *outs):
    for step, out in enumerate(outs):
        near = own[step].astype(f32) + pair[step].astype(f32)
        far = beside[step].astype(f32) + across[step].astype(f32)
        out[...] = (near + far).astype(bf16)


def weights_kernel(terms, total):
    summed = terms[0].astype(f32)
    for piece in range(1, terms.shape[0]):
        summed += terms[piece].astype(f32)
    for piece in range(total.shape[0]):
        total[piece] = summed


def result_kernel(*refs):
    terms, (w_msg, gathered, grad, grad_w_msg, grad_w_out) = refs[:-5], refs[-5:]
    lanes = gathered.shape[2]
    summed = terms[0][...].astype(f32)
    for term in terms[1:]:
        summed += term[...].astype(f32)
    grad[...] = lax.dot_general(
        summed.astype(bf16), w_msg[...], (((0,), (1,)), ((), ())), preferred_element_type=f32
    ).astype(bf16)
    for quarter, out in enumerate((grad_w_out, grad_w_out, grad_w_msg, grad_w_msg)):
        at = quarter % 2 * lanes
        out[:, at : at + lanes] = gathered[quarter]


def in_vmem(count):
    return [pl.BlockSpec(memory_space=pltpu.VMEM)] * count


def in_smem(count):
    return [pl.BlockSpec(memory_space=pltpu.SMEM)] * count


def limits(mebibytes):
    return pltpu.CompilerParams(vmem_limit_bytes=mebibytes * 2**20)


def per_device(features, cotangent, w_msg, w_out, tile_vals, tile_emit, tile_recv, tile_count):
    own_rows = features[0]
    facet_rows, width = own_rows.shape
    tile_dim = tile_vals.shape[-1]
    emit_size = lax.axis_size("emit")
    recv_size = lax.axis_size("recv")
    recv_blocks = facet_rows * emit_size // tile_dim
    emit_blocks = facet_rows * recv_size // tile_dim
    chips = emit_size // 2
    lanes = width // 2
    values = tile_vals[0, 0]
    steps = recv_size // 4
    recv_at = lax.axis_index("recv")
    column, parity = lax.rem(recv_at, 2), lax.rem(lax.div(recv_at, 2), 2)
    core = lax.rem(lax.axis_index("emit"), 2)
    numbers = jnp.concatenate(
        [
            tile_count[0],
            jnp.stack([core, column, parity, lax.div(recv_at, 4)]),
            tile_emit[0, 0],
            tile_recv[0, 0],
        ]
    )
    same_core = [list(range(parity, emit_size, 2)) for parity in range(2)]
    swap = [(member, member ^ 1) for member in range(emit_size)]
    struct = jax.ShapeDtypeStruct
    in_hbm = pl.BlockSpec(memory_space=pltpu.HBM)
    sweep_scratch = [
        pltpu.VMEM((ring_depth, group_tiles, tile_dim, tile_dim), bf16),
        pltpu.SemaphoreType.DMA((ring_depth,)),
    ]

    second_core = jnp.broadcast_to(core.astype(f32), (8, lanes))
    sweep_cost = pl.CostEstimate(
        flops=2 * values.size * width, bytes_accessed=2 * values.size, transcendentals=0
    )

    def to_quad(array, bits):
        return lax.ppermute(array, "recv", [(member, member ^ bits) for member in range(recv_size)])

    def along_z(array, step):
        return lax.ppermute(
            array, "recv", [(member, (member + 4 * step) % recv_size) for member in range(recv_size)]
        )

    arrivals = {step: along_z(own_rows, step) for step in sorted(range(1, steps), key=lambda step: abs(2 * step - steps))}
    held_rows = pl.pallas_call(
        copy_kernel,
        out_shape=struct(own_rows.shape, bf16),
        in_specs=in_vmem(1),
        out_specs=in_vmem(1)[0],
        compiler_params=limits(8),
        name="own_rows",
    )(own_rows)
    column_rows = jnp.stack([held_rows] + [arrivals[step] for step in range(1, steps)])
    kept, sent = pl.pallas_call(
        forward_kernel,
        out_shape=(
            struct((recv_blocks, tile_dim // 2, width), f32),
            struct((recv_blocks, tile_dim // 2, width), bf16),
        ),
        in_specs=in_smem(1) + in_vmem(4) + [in_hbm],
        out_specs=tuple(in_vmem(2)),
        scratch_shapes=[
            pltpu.VMEM((emit_blocks, tile_dim, width), bf16),
            pltpu.VMEM((recv_blocks + 1, tile_dim, width), f32),
        ]
        + sweep_scratch,
        compiler_params=limits(48),
        cost_estimate=sweep_cost,
        name="forward_sweep",
    )(
        numbers,
        column_rows,
        to_quad(column_rows, 2),
        to_quad(column_rows, 1),
        to_quad(column_rows, 3),
        values,
    )
    arrived = lax.ppermute(sent, "emit", swap)
    pair_sum = (kept + arrived.astype(f32)).astype(bf16)
    terms = lax.all_to_all(pair_sum, "emit", 0, 0, tiled=True, axis_index_groups=same_core)

    chunk = 4 * width // chips
    payload = pl.pallas_call(
        middle_kernel,
        out_shape=struct((chips, width + chunk, lanes), bf16),
        in_specs=in_vmem(4),
        out_specs=in_vmem(1)[0],
        compiler_params=limits(16),
        name="middle",
    )(terms, cotangent[0], w_msg, w_out)
    held = lax.all_to_all(payload, "emit", 0, 0, tiled=True, axis_index_groups=same_core)
    other = lax.ppermute(held, "emit", swap)

    weights = pl.pallas_call(
        chunk_kernel,
        out_shape=struct((recv_size, chunk // 2, lanes), bf16),
        in_specs=in_vmem(3),
        out_specs=in_vmem(1)[0],
        compiler_params=limits(8),
        name="weights_chunk",
    )(held, other, second_core)
    chunks = lax.all_to_all(weights, "recv", 0, 0, tiled=True)

    own, pair, beside, across = pl.pallas_call(
        backward_kernel,
        out_shape=(struct((steps, width, lanes), bf16),) * 4,
        in_specs=in_smem(1) + in_vmem(2) + [in_hbm],
        out_specs=tuple(in_vmem(4)),
        scratch_shapes=[
            pltpu.VMEM((recv_blocks, width, tile_dim), bf16),
            pltpu.VMEM((emit_blocks + 1, width, tile_dim), f32),
        ]
        + sweep_scratch,
        compiler_params=limits(48),
        cost_estimate=sweep_cost,
        name="backward_sweep",
    )(numbers, held, other, values)
    terms = pl.pallas_call(
        quad_kernel,
        out_shape=(struct((width, lanes), bf16),) * steps,
        in_specs=in_vmem(4),
        out_specs=tuple(in_vmem(steps)),
        compiler_params=limits(8),
        name="quad_sum",
    )(own, to_quad(pair, 2), to_quad(beside, 1), to_quad(across, 3))
    chunks, terms = lax.optimization_barrier((chunks, terms))

    total = pl.pallas_call(
        weights_kernel,
        out_shape=struct((emit_size, chunk // 2, lanes), f32),
        in_specs=in_vmem(1),
        out_specs=in_vmem(1)[0],
        compiler_params=limits(8),
        name="weights_sum",
    )(chunks)
    gathered = lax.all_to_all(total, "emit", 0, 0, tiled=True).reshape(4, width, lanes)
    terms = [terms[0]] + [along_z(terms[step], step) for step in range(1, steps)]
    grad_features, grad_w_msg, grad_w_out = pl.pallas_call(
        result_kernel,
        out_shape=(
            struct((facet_rows, width), bf16),
            struct((width, width), f32),
            struct((width, width), f32),
        ),
        in_specs=in_vmem(steps + 2),
        out_specs=tuple(in_vmem(3)),
        compiler_params=limits(8),
        name="results",
    )(*terms, w_msg, gathered)
    return (grad_features[None], grad_w_msg, grad_w_out)


def solution(mesh):
    in_specs = (
        P("emit", "recv", None),
        P("recv", "emit", None),
        P(),
        P(),
        P("emit", "recv", None, None, None),
        P("emit", "recv", None),
        P("emit", "recv", None),
        P("emit", "recv"),
    )
    out_specs = (P("emit", "recv", None), P(), P())
    return jax.shard_map(
        per_device, mesh=mesh, in_specs=in_specs, out_specs=out_specs, check_vma=False
    )
```

```python
import jax
import jax.numpy as jnp
from jax import lax
from jax.experimental import pallas as pl
from jax.experimental.pallas import tpu as pltpu
from jax.sharding import PartitionSpec as P

ring_depth = 8
group_tiles = 8
f32 = jnp.float32
bf16 = jnp.bfloat16


def add_group(first, live, tiles, product, target, acc):
    spare = acc.shape[0] - 1
    slots = [first + at for at in range(group_tiles)]
    products = [product(slot, tiles[at]) for at, slot in enumerate(slots)]
    for slot, term in zip(slots, products):
        acc[jnp.where(slot < live, target(slot), spare)] += term


def sweep(live, tiles, ring, sems, prepare, product, target, acc):
    depth = ring.shape[0]
    steps = lax.div(live + group_tiles - 1, group_tiles)

    def copy(step):
        place = lax.rem(step, depth)
        return pltpu.make_async_copy(
            tiles.at[pl.ds(step * group_tiles, group_tiles)], ring.at[place], sems.at[place]
        )

    def begin(step, carry):
        copy(step).start()
        return carry

    lax.fori_loop(0, jnp.minimum(steps, depth), begin, 0)
    acc[...] = jnp.zeros_like(acc)
    prepare()

    def advance(step, carry):
        copy(step).wait()
        held = ring.at[lax.rem(step, depth)]
        add_group(step * group_tiles, live, held, product, target, acc)

        @pl.when(step + depth < steps)
        def _():
            copy(step + depth).start()

        return carry

    lax.fori_loop(0, steps, advance, 0)


def unpack(numbers, slots):
    return *(numbers[at] for at in range(5)), lambda slot: numbers[5 + slot], lambda slot: numbers[5 + slots + slot]


def forward_kernel(
    numbers, own, pair, beside, across, tiles, kept, sent, rows, acc, ring, sems
):
    half = kept.shape[1]
    live, core, column, parity, height, emit_block, recv_block = unpack(numbers, tiles.shape[0])

    def prepare():
        for held, side, odd in (
            (own, column, parity),
            (pair, column, 1 - parity),
            (beside, 1 - column, parity),
            (across, 1 - column, 1 - parity),
        ):
            at = pl.ds(pl.multiple_of(side * half, half), half)
            steps = held.shape[0]
            for step in range(steps):
                rows[2 * lax.rem(height + steps - step, steps) + odd, at, :] = held[step]

    def product(slot, tile):
        return jnp.dot(tile, rows[emit_block(slot)], preferred_element_type=f32)

    sweep(live, tiles, ring, sems, prepare, product, recv_block, acc)
    mine = pl.multiple_of(core * half, half)
    other = pl.multiple_of((1 - core) * half, half)
    for block in range(kept.shape[0]):
        sent[block] = acc[block, pl.ds(other, half), :].astype(bf16)
        kept[block] = acc[block, pl.ds(mine, half), :]


def middle_kernel(terms, cotangent, w_msg, w_out, payload):
    width = w_msg.shape[0]
    pieces = terms.shape[0]
    lanes = width // 2
    summed = terms[0].astype(f32)
    for piece in range(1, pieces):
        summed += terms[piece].astype(f32)
    summed = summed.astype(bf16)
    message = jnp.dot(summed, w_msg[...], preferred_element_type=f32).astype(bf16)
    preact = jnp.dot(message, w_out[...], preferred_element_type=f32)
    sigmoid_pre = jax.nn.sigmoid(preact)
    slope = sigmoid_pre * (1.0 + preact * (1.0 - sigmoid_pre))
    grad_preact = (cotangent[...].astype(f32) * slope).astype(bf16)
    across = (((1,), (1,)), ((), ()))
    along = (((0,), (0,)), ((), ()))
    grad_turned = lax.dot_general(w_out[...], grad_preact, across, preferred_element_type=f32).astype(bf16)
    grad = lax.dot_general(grad_preact, w_out[...], across, preferred_element_type=f32).astype(bf16)
    out_part = lax.dot_general(message, grad_preact, along, preferred_element_type=f32).astype(bf16)
    msg_part = lax.dot_general(summed, grad, along, preferred_element_type=f32).astype(bf16)
    parts = (
        out_part[:, :lanes],
        out_part[:, lanes:],
        msg_part[:, :lanes],
        msg_part[:, lanes:],
    )
    chunk = 4 * width // pieces
    for piece in range(pieces):
        payload[piece, :width, :] = grad_turned
        at = 0
        while at < chunk:
            quarter, row = divmod(piece * chunk + at, width)
            size = min(chunk - at, width - row)
            payload[piece, width + at : width + at + size, :] = parts[quarter][row : row + size]
            at += size


def backward_kernel(
    numbers, held, other, tiles, own, pair, beside, across, grads, acc, ring, sems
):
    live, core, column, parity, height, emit_block, recv_block = unpack(numbers, tiles.shape[0])
    width, lanes = acc.shape[1], held.shape[2]
    steps = own.shape[0]

    def lay(first, second):
        for block in range(held.shape[0]):
            grads[block, :, :lanes] = first[block, :width, :]
            grads[block, :, lanes:] = second[block, :width, :]

    def prepare():
        @pl.when(core == 0)
        def _():
            lay(held, other)

        @pl.when(core == 1)
        def _():
            lay(other, held)

    def product(slot, tile):
        return jnp.dot(grads[recv_block(slot)], tile, preferred_element_type=f32)

    sweep(live, tiles, ring, sems, prepare, product, emit_block, acc)
    def hand_out(near):
        for out, side, odd in (
            (own, near, parity),
            (pair, near, 1 - parity),
            (beside, 1 - near, parity),
            (across, 1 - near, 1 - parity),
        ):
            for step in range(steps):
                at = 2 * lax.rem(height + step, steps) + odd
                block = acc[at, :, side * lanes : (side + 1) * lanes]
                out[step] = block.astype(bf16)

    @pl.when(column == 0)
    def _():
        hand_out(0)

    @pl.when(column == 1)
    def _():
        hand_out(1)


def copy_kernel(source, out):
    out[...] = source[...]


def chunk_kernel(held, other, second_core, out):
    chunk = out.shape[1]
    width = held.shape[1] - 2 * chunk

    def summed(rows):
        total = held[0, rows, :].astype(f32) + other[0, rows, :].astype(f32)
        for block in range(1, held.shape[0]):
            total += held[block, rows, :].astype(f32) + other[block, rows, :].astype(f32)
        return total

    first, second = summed(slice(width, width + chunk)), summed(slice(width + chunk, None))
    mine = jnp.where(second_core[0:1, :] > 0.5, second, first).astype(bf16)
    for piece in range(out.shape[0]):
        out[piece] = mine


def quad_kernel(own, pair, beside, across, *outs):
    for step, out in enumerate(outs):
        near = own[step].astype(f32) + pair[step].astype(f32)
        far = beside[step].astype(f32) + across[step].astype(f32)
        out[...] = (near + far).astype(bf16)


def weights_kernel(terms, total):
    summed = terms[0].astype(f32)
    for piece in range(1, terms.shape[0]):
        summed += terms[piece].astype(f32)
    for piece in range(total.shape[0]):
        total[piece] = summed


def features_kernel(*refs):
    terms, w_msg, grad = refs[:-2], refs[-2], refs[-1]
    summed = terms[0][...].astype(f32)
    for term in terms[1:]:
        summed += term[...].astype(f32)
    grad[...] = lax.dot_general(
        summed.astype(bf16), w_msg[...], (((0,), (1,)), ((), ())), preferred_element_type=f32
    ).astype(bf16)


def in_vmem(count):
    return [pl.BlockSpec(memory_space=pltpu.VMEM)] * count


def in_smem(count):
    return [pl.BlockSpec(memory_space=pltpu.SMEM)] * count


def limits(mebibytes):
    return pltpu.CompilerParams(vmem_limit_bytes=mebibytes * 2**20)


def per_device(features, cotangent, w_msg, w_out, tile_vals, tile_emit, tile_recv, tile_count):
    own_rows = features[0]
    facet_rows, width = own_rows.shape
    tile_dim = tile_vals.shape[-1]
    emit_size = lax.axis_size("emit")
    recv_size = lax.axis_size("recv")
    recv_blocks = facet_rows * emit_size // tile_dim
    emit_blocks = facet_rows * recv_size // tile_dim
    chips = emit_size // 2
    lanes = width // 2
    values = tile_vals[0, 0]
    steps = recv_size // 4
    recv_at = lax.axis_index("recv")
    column, parity = lax.rem(recv_at, 2), lax.rem(lax.div(recv_at, 2), 2)
    core = lax.rem(lax.axis_index("emit"), 2)
    numbers = jnp.concatenate(
        [
            tile_count[0],
            jnp.stack([core, column, parity, lax.div(recv_at, 4)]),
            tile_emit[0, 0],
            tile_recv[0, 0],
        ]
    )
    same_core = [list(range(parity, emit_size, 2)) for parity in range(2)]
    swap = [(member, member ^ 1) for member in range(emit_size)]
    struct = jax.ShapeDtypeStruct
    in_hbm = pl.BlockSpec(memory_space=pltpu.HBM)
    sweep_scratch = [
        pltpu.VMEM((ring_depth, group_tiles, tile_dim, tile_dim), bf16),
        pltpu.SemaphoreType.DMA((ring_depth,)),
    ]

    second_core = jnp.broadcast_to(core.astype(f32), (8, lanes))
    rated_long = pl.CostEstimate(flops=2**37, bytes_accessed=2**24, transcendentals=0)
    sweep_cost = pl.CostEstimate(
        flops=2 * values.size * width, bytes_accessed=2 * values.size, transcendentals=0
    )

    def to_quad(array, bits):
        return lax.ppermute(array, "recv", [(member, member ^ bits) for member in range(recv_size)])

    def along_z(array, step):
        return lax.ppermute(
            array, "recv", [(member, (member + 4 * step) % recv_size) for member in range(recv_size)]
        )

    arrivals = {step: along_z(own_rows, step) for step in sorted(range(1, steps), key=lambda step: abs(2 * step - steps))}
    held_rows = pl.pallas_call(
        copy_kernel,
        out_shape=struct(own_rows.shape, bf16),
        in_specs=in_vmem(1),
        out_specs=in_vmem(1)[0],
        compiler_params=limits(8),
        name="own_rows",
    )(own_rows)
    column_rows = jnp.stack([held_rows] + [arrivals[step] for step in range(1, steps)])
    kept, sent = pl.pallas_call(
        forward_kernel,
        out_shape=(
            struct((recv_blocks, tile_dim // 2, width), f32),
            struct((recv_blocks, tile_dim // 2, width), bf16),
        ),
        in_specs=in_smem(1) + in_vmem(4) + [in_hbm],
        out_specs=tuple(in_vmem(2)),
        scratch_shapes=[
            pltpu.VMEM((emit_blocks, tile_dim, width), bf16),
            pltpu.VMEM((recv_blocks + 1, tile_dim, width), f32),
        ]
        + sweep_scratch,
        compiler_params=limits(48),
        cost_estimate=sweep_cost,
        name="forward_sweep",
    )(
        numbers,
        column_rows,
        to_quad(column_rows, 2),
        to_quad(column_rows, 1),
        to_quad(column_rows, 3),
        values,
    )
    arrived = lax.ppermute(sent, "emit", swap)
    pair_sum = (kept + arrived.astype(f32)).astype(bf16)
    terms = lax.all_to_all(pair_sum, "emit", 0, 0, tiled=True, axis_index_groups=same_core)

    chunk = 4 * width // chips
    payload = pl.pallas_call(
        middle_kernel,
        out_shape=struct((chips, width + chunk, lanes), bf16),
        in_specs=in_vmem(4),
        out_specs=in_vmem(1)[0],
        compiler_params=limits(16),
        name="middle",
    )(terms, cotangent[0], w_msg, w_out)
    held = lax.all_to_all(payload, "emit", 0, 0, tiled=True, axis_index_groups=same_core)
    other = lax.ppermute(held, "emit", swap)

    own, pair, beside, across = pl.pallas_call(
        backward_kernel,
        out_shape=(struct((steps, width, lanes), bf16),) * 4,
        in_specs=in_smem(1) + in_vmem(2) + [in_hbm],
        out_specs=tuple(in_vmem(4)),
        scratch_shapes=[
            pltpu.VMEM((recv_blocks, width, tile_dim), bf16),
            pltpu.VMEM((emit_blocks + 1, width, tile_dim), f32),
        ]
        + sweep_scratch,
        compiler_params=limits(48),
        cost_estimate=sweep_cost,
        name="backward_sweep",
    )(numbers, held, other, values)
    own, held, other = lax.optimization_barrier((own, held, other))
    weights = pl.pallas_call(
        chunk_kernel,
        out_shape=struct((recv_size, chunk // 2, lanes), bf16),
        in_specs=in_vmem(3),
        out_specs=in_vmem(1)[0],
        compiler_params=limits(8),
        name="weights_chunk",
    )(held, other, second_core)
    chunks = lax.all_to_all(weights, "recv", 0, 0, tiled=True)

    terms = pl.pallas_call(
        quad_kernel,
        out_shape=(struct((width, lanes), bf16),) * steps,
        in_specs=in_vmem(4),
        out_specs=tuple(in_vmem(steps)),
        compiler_params=limits(8),
        cost_estimate=rated_long,
        name="quad_sum",
    )(own, to_quad(pair, 2), to_quad(beside, 1), to_quad(across, 3))
    chunks, _ = lax.optimization_barrier((chunks, terms[0]))

    total = pl.pallas_call(
        weights_kernel,
        out_shape=struct((emit_size, chunk // 2, lanes), f32),
        in_specs=in_vmem(1),
        out_specs=in_vmem(1)[0],
        compiler_params=limits(8),
        name="weights_sum",
    )(chunks)
    gathered = lax.all_to_all(total, "emit", 0, 0, tiled=True).reshape(4, width, lanes)
    terms = [terms[0]] + [along_z(terms[step], step) for step in range(1, steps)]
    grad_features = pl.pallas_call(
        features_kernel,
        out_shape=struct((facet_rows, width), bf16),
        in_specs=in_vmem(steps + 1),
        out_specs=in_vmem(1)[0],
        compiler_params=limits(8),
        cost_estimate=rated_long,
        name="features_grad",
    )(*terms, w_msg)[None]
    grad_w_out = jnp.concatenate([gathered[0], gathered[1]], axis=1)
    grad_w_msg = jnp.concatenate([gathered[2], gathered[3]], axis=1)
    return (grad_features, grad_w_msg, grad_w_out)


def solution(mesh):
    in_specs = (
        P("emit", "recv", None),
        P("recv", "emit", None),
        P(),
        P(),
        P("emit", "recv", None, None, None),
        P("emit", "recv", None),
        P("emit", "recv", None),
        P("emit", "recv"),
    )
    out_specs = (P("emit", "recv", None), P(), P())
    return jax.shard_map(
        per_device, mesh=mesh, in_specs=in_specs, out_specs=out_specs, check_vma=False
    )
```

```python
import jax
import jax.numpy as jnp
from jax import lax
from jax.experimental import pallas as pl
from jax.experimental.pallas import tpu as pltpu
from jax.sharding import PartitionSpec as P

ring_depth = 8
group_tiles = 8
f32 = jnp.float32
bf16 = jnp.bfloat16


def add_group(first, live, tiles, product, target, acc):
    spare = acc.shape[0] - 1
    slots = [first + at for at in range(group_tiles)]
    products = [product(slot, tiles[at]) for at, slot in enumerate(slots)]
    for slot, term in zip(slots, products):
        acc[jnp.where(slot < live, target(slot), spare)] += term


def sweep(live, tiles, ring, sems, prepare, product, target, acc):
    depth = ring.shape[0]
    steps = lax.div(live + group_tiles - 1, group_tiles)

    def copy(step):
        place = lax.rem(step, depth)
        return pltpu.make_async_copy(
            tiles.at[pl.ds(step * group_tiles, group_tiles)], ring.at[place], sems.at[place]
        )

    def begin(step, carry):
        copy(step).start()
        return carry

    lax.fori_loop(0, jnp.minimum(steps, depth), begin, 0)
    acc[...] = jnp.zeros_like(acc)
    prepare()

    def advance(step, carry):
        copy(step).wait()
        held = ring.at[lax.rem(step, depth)]
        add_group(step * group_tiles, live, held, product, target, acc)

        @pl.when(step + depth < steps)
        def _():
            copy(step + depth).start()

        return carry

    lax.fori_loop(0, steps, advance, 0)


def unpack(numbers, slots):
    return *(numbers[at] for at in range(5)), lambda slot: numbers[5 + slot], lambda slot: numbers[5 + slots + slot]


def forward_kernel(
    numbers, own, pair, beside, across, tiles, kept, sent, rows, acc, ring, sems
):
    half = kept.shape[1]
    live, core, column, parity, height, emit_block, recv_block = unpack(numbers, tiles.shape[0])

    def prepare():
        for held, side, odd in (
            (own, column, parity),
            (pair, column, 1 - parity),
            (beside, 1 - column, parity),
            (across, 1 - column, 1 - parity),
        ):
            at = pl.ds(pl.multiple_of(side * half, half), half)
            steps = held.shape[0]
            for step in range(steps):
                rows[2 * lax.rem(height + steps - step, steps) + odd, at, :] = held[step]

    def product(slot, tile):
        return jnp.dot(tile, rows[emit_block(slot)], preferred_element_type=f32)

    sweep(live, tiles, ring, sems, prepare, product, recv_block, acc)
    mine = pl.multiple_of(core * half, half)
    other = pl.multiple_of((1 - core) * half, half)
    for block in range(kept.shape[0]):
        sent[block] = acc[block, pl.ds(other, half), :].astype(bf16)
        kept[block] = acc[block, pl.ds(mine, half), :]


def middle_kernel(terms, cotangent, w_msg, w_out, payload):
    width = w_msg.shape[0]
    pieces = terms.shape[0]
    lanes = width // 2
    summed = terms[0].astype(f32)
    for piece in range(1, pieces):
        summed += terms[piece].astype(f32)
    summed = summed.astype(bf16)
    message = jnp.dot(summed, w_msg[...], preferred_element_type=f32).astype(bf16)
    preact = jnp.dot(message, w_out[...], preferred_element_type=f32)
    sigmoid_pre = jax.nn.sigmoid(preact)
    slope = sigmoid_pre * (1.0 + preact * (1.0 - sigmoid_pre))
    grad_preact = (cotangent[...].astype(f32) * slope).astype(bf16)
    across = (((1,), (1,)), ((), ()))
    along = (((0,), (0,)), ((), ()))
    grad_turned = lax.dot_general(w_out[...], grad_preact, across, preferred_element_type=f32).astype(bf16)
    grad = lax.dot_general(grad_preact, w_out[...], across, preferred_element_type=f32).astype(bf16)
    out_part = lax.dot_general(message, grad_preact, along, preferred_element_type=f32).astype(bf16)
    msg_part = lax.dot_general(summed, grad, along, preferred_element_type=f32).astype(bf16)
    parts = (
        out_part[:, :lanes],
        out_part[:, lanes:],
        msg_part[:, :lanes],
        msg_part[:, lanes:],
    )
    chunk = 4 * width // pieces
    for piece in range(pieces):
        payload[piece, :width, :] = grad_turned
        at = 0
        while at < chunk:
            quarter, row = divmod(piece * chunk + at, width)
            size = min(chunk - at, width - row)
            payload[piece, width + at : width + at + size, :] = parts[quarter][row : row + size]
            at += size


def backward_kernel(
    numbers, held, other, tiles, own, pair, beside, across, grads, acc, ring, sems
):
    live, core, column, parity, height, emit_block, recv_block = unpack(numbers, tiles.shape[0])
    width, lanes = acc.shape[1], held.shape[2]
    steps = own.shape[0]

    def lay(first, second):
        for block in range(held.shape[0]):
            grads[block, :, :lanes] = first[block, :width, :]
            grads[block, :, lanes:] = second[block, :width, :]

    def prepare():
        @pl.when(core == 0)
        def _():
            lay(held, other)

        @pl.when(core == 1)
        def _():
            lay(other, held)

    def product(slot, tile):
        return jnp.dot(grads[recv_block(slot)], tile, preferred_element_type=f32)

    sweep(live, tiles, ring, sems, prepare, product, emit_block, acc)
    def hand_out(near):
        for out, side, odd in (
            (own, near, parity),
            (pair, near, 1 - parity),
            (beside, 1 - near, parity),
            (across, 1 - near, 1 - parity),
        ):
            for step in range(steps):
                at = 2 * lax.rem(height + step, steps) + odd
                block = acc[at, :, side * lanes : (side + 1) * lanes]
                out[step] = block.astype(bf16)

    @pl.when(column == 0)
    def _():
        hand_out(0)

    @pl.when(column == 1)
    def _():
        hand_out(1)


def copy_kernel(source, out):
    out[...] = source[...]


def chunk_kernel(held, other, second_core, out):
    chunk = out.shape[1]
    width = held.shape[1] - 2 * chunk

    def summed(rows):
        total = held[0, rows, :].astype(f32) + other[0, rows, :].astype(f32)
        for block in range(1, held.shape[0]):
            total += held[block, rows, :].astype(f32) + other[block, rows, :].astype(f32)
        return total

    first, second = summed(slice(width, width + chunk)), summed(slice(width + chunk, None))
    mine = jnp.where(second_core[0:1, :] > 0.5, second, first).astype(bf16)
    for piece in range(out.shape[0]):
        out[piece] = mine


def quad_kernel(own, pair, beside, across, *outs):
    for step, out in enumerate(outs):
        near = own[step].astype(f32) + pair[step].astype(f32)
        far = beside[step].astype(f32) + across[step].astype(f32)
        out[...] = (near + far).astype(bf16)


def weights_kernel(terms, total):
    summed = terms[0].astype(f32)
    for piece in range(1, terms.shape[0]):
        summed += terms[piece].astype(f32)
    for piece in range(total.shape[0]):
        total[piece] = summed


def result_kernel(*refs):
    terms, (w_msg, gathered, grad, grad_w_msg, grad_w_out) = refs[:-5], refs[-5:]
    lanes = gathered.shape[2]
    summed = terms[0][...].astype(f32)
    for term in terms[1:]:
        summed += term[...].astype(f32)
    grad[...] = lax.dot_general(
        summed.astype(bf16), w_msg[...], (((0,), (1,)), ((), ())), preferred_element_type=f32
    ).astype(bf16)
    for quarter, out in enumerate((grad_w_out, grad_w_out, grad_w_msg, grad_w_msg)):
        at = quarter % 2 * lanes
        out[:, at : at + lanes] = gathered[quarter]


def in_vmem(count):
    return [pl.BlockSpec(memory_space=pltpu.VMEM)] * count


def in_smem(count):
    return [pl.BlockSpec(memory_space=pltpu.SMEM)] * count


def limits(mebibytes):
    return pltpu.CompilerParams(vmem_limit_bytes=mebibytes * 2**20)


def per_device(features, cotangent, w_msg, w_out, tile_vals, tile_emit, tile_recv, tile_count):
    own_rows = features[0]
    facet_rows, width = own_rows.shape
    tile_dim = tile_vals.shape[-1]
    emit_size = lax.axis_size("emit")
    recv_size = lax.axis_size("recv")
    recv_blocks = facet_rows * emit_size // tile_dim
    emit_blocks = facet_rows * recv_size // tile_dim
    chips = emit_size // 2
    lanes = width // 2
    values = tile_vals[0, 0]
    steps = recv_size // 4
    recv_at = lax.axis_index("recv")
    column, parity = lax.rem(recv_at, 2), lax.rem(lax.div(recv_at, 2), 2)
    core = lax.rem(lax.axis_index("emit"), 2)
    numbers = jnp.concatenate(
        [
            tile_count[0],
            jnp.stack([core, column, parity, lax.div(recv_at, 4)]),
            tile_emit[0, 0],
            tile_recv[0, 0],
        ]
    )
    same_core = [list(range(parity, emit_size, 2)) for parity in range(2)]
    swap = [(member, member ^ 1) for member in range(emit_size)]
    struct = jax.ShapeDtypeStruct
    in_hbm = pl.BlockSpec(memory_space=pltpu.HBM)
    sweep_scratch = [
        pltpu.VMEM((ring_depth, group_tiles, tile_dim, tile_dim), bf16),
        pltpu.SemaphoreType.DMA((ring_depth,)),
    ]

    second_core = jnp.broadcast_to(core.astype(f32), (8, lanes))
    rated_long = pl.CostEstimate(flops=2**37, bytes_accessed=2**24, transcendentals=0)
    sweep_cost = pl.CostEstimate(
        flops=2 * values.size * width, bytes_accessed=2 * values.size, transcendentals=0
    )

    def to_quad(array, bits):
        return lax.ppermute(array, "recv", [(member, member ^ bits) for member in range(recv_size)])

    def along_z(array, step):
        return lax.ppermute(
            array, "recv", [(member, (member + 4 * step) % recv_size) for member in range(recv_size)]
        )

    arrivals = {step: along_z(own_rows, step) for step in sorted(range(1, steps), key=lambda step: abs(2 * step - steps))}
    held_rows = pl.pallas_call(
        copy_kernel,
        out_shape=struct(own_rows.shape, bf16),
        in_specs=in_vmem(1),
        out_specs=in_vmem(1)[0],
        compiler_params=limits(8),
        name="own_rows",
    )(own_rows)
    column_rows = jnp.stack([held_rows] + [arrivals[step] for step in range(1, steps)])
    kept, sent = pl.pallas_call(
        forward_kernel,
        out_shape=(
            struct((recv_blocks, tile_dim // 2, width), f32),
            struct((recv_blocks, tile_dim // 2, width), bf16),
        ),
        in_specs=in_smem(1) + in_vmem(4) + [in_hbm],
        out_specs=tuple(in_vmem(2)),
        scratch_shapes=[
            pltpu.VMEM((emit_blocks, tile_dim, width), bf16),
            pltpu.VMEM((recv_blocks + 1, tile_dim, width), f32),
        ]
        + sweep_scratch,
        compiler_params=limits(48),
        cost_estimate=sweep_cost,
        name="forward_sweep",
    )(
        numbers,
        column_rows,
        to_quad(column_rows, 2),
        to_quad(column_rows, 1),
        to_quad(column_rows, 3),
        values,
    )
    arrived = lax.ppermute(sent, "emit", swap)
    pair_sum = (kept + arrived.astype(f32)).astype(bf16)
    terms = lax.all_to_all(pair_sum, "emit", 0, 0, tiled=True, axis_index_groups=same_core)

    chunk = 4 * width // chips
    payload = pl.pallas_call(
        middle_kernel,
        out_shape=struct((chips, width + chunk, lanes), bf16),
        in_specs=in_vmem(4),
        out_specs=in_vmem(1)[0],
        compiler_params=limits(16),
        name="middle",
    )(terms, cotangent[0], w_msg, w_out)
    held = lax.all_to_all(payload, "emit", 0, 0, tiled=True, axis_index_groups=same_core)
    other = lax.ppermute(held, "emit", swap)

    own, pair, beside, across = pl.pallas_call(
        backward_kernel,
        out_shape=(struct((steps, width, lanes), bf16),) * 4,
        in_specs=in_smem(1) + in_vmem(2) + [in_hbm],
        out_specs=tuple(in_vmem(4)),
        scratch_shapes=[
            pltpu.VMEM((recv_blocks, width, tile_dim), bf16),
            pltpu.VMEM((emit_blocks + 1, width, tile_dim), f32),
        ]
        + sweep_scratch,
        compiler_params=limits(48),
        cost_estimate=sweep_cost,
        name="backward_sweep",
    )(numbers, held, other, values)
    own, held, other = lax.optimization_barrier((own, held, other))
    weights = pl.pallas_call(
        chunk_kernel,
        out_shape=struct((recv_size, chunk // 2, lanes), bf16),
        in_specs=in_vmem(3),
        out_specs=in_vmem(1)[0],
        compiler_params=limits(8),
        name="weights_chunk",
    )(held, other, second_core)
    chunks = lax.all_to_all(weights, "recv", 0, 0, tiled=True)

    terms = pl.pallas_call(
        quad_kernel,
        out_shape=(struct((width, lanes), bf16),) * steps,
        in_specs=in_vmem(4),
        out_specs=tuple(in_vmem(steps)),
        compiler_params=limits(8),
        cost_estimate=rated_long,
        name="quad_sum",
    )(own, to_quad(pair, 2), to_quad(beside, 1), to_quad(across, 3))
    chunks, terms = lax.optimization_barrier((chunks, terms))

    total = pl.pallas_call(
        weights_kernel,
        out_shape=struct((emit_size, chunk // 2, lanes), f32),
        in_specs=in_vmem(1),
        out_specs=in_vmem(1)[0],
        compiler_params=limits(8),
        name="weights_sum",
    )(chunks)
    gathered = lax.all_to_all(total, "emit", 0, 0, tiled=True).reshape(4, width, lanes)
    terms = [terms[0]] + [along_z(terms[step], step) for step in range(1, steps)]
    grad_features, grad_w_msg, grad_w_out = pl.pallas_call(
        result_kernel,
        out_shape=(
            struct((facet_rows, width), bf16),
            struct((width, width), f32),
            struct((width, width), f32),
        ),
        in_specs=in_vmem(steps + 2),
        out_specs=tuple(in_vmem(3)),
        compiler_params=limits(8),
        name="results",
    )(*terms, w_msg, gathered)
    return (grad_features[None], grad_w_msg, grad_w_out)


def solution(mesh):
    in_specs = (
        P("emit", "recv", None),
        P("recv", "emit", None),
        P(),
        P(),
        P("emit", "recv", None, None, None),
        P("emit", "recv", None),
        P("emit", "recv", None),
        P("emit", "recv"),
    )
    out_specs = (P("emit", "recv", None), P(), P())
    return jax.shard_map(
        per_device, mesh=mesh, in_specs=in_specs, out_specs=out_specs, check_vma=False
    )
```

```python
import jax
import jax.numpy as jnp
from jax import lax
from jax.experimental import pallas as pl
from jax.experimental.pallas import tpu as pltpu
from jax.sharding import PartitionSpec as P

ring_depth = 8
group_tiles = 8
f32 = jnp.float32
bf16 = jnp.bfloat16


def add_group(first, live, tiles, product, target, acc):
    spare = acc.shape[0] - 1
    slots = [first + at for at in range(group_tiles)]
    products = [product(slot, tiles[at]) for at, slot in enumerate(slots)]
    for slot, term in zip(slots, products):
        acc[jnp.where(slot < live, target(slot), spare)] += term


def sweep(live, tiles, ring, sems, prepare, product, target, acc):
    depth = ring.shape[0]
    steps = lax.div(live + group_tiles - 1, group_tiles)

    def copy(step):
        place = lax.rem(step, depth)
        return pltpu.make_async_copy(
            tiles.at[pl.ds(step * group_tiles, group_tiles)], ring.at[place], sems.at[place]
        )

    def begin(step, carry):
        copy(step).start()
        return carry

    lax.fori_loop(0, jnp.minimum(steps, depth), begin, 0)
    acc[...] = jnp.zeros_like(acc)
    prepare()

    def advance(step, carry):
        copy(step).wait()
        held = ring.at[lax.rem(step, depth)]
        add_group(step * group_tiles, live, held, product, target, acc)

        @pl.when(step + depth < steps)
        def _():
            copy(step + depth).start()

        return carry

    lax.fori_loop(0, steps, advance, 0)


def unpack(numbers, slots):
    return *(numbers[at] for at in range(5)), lambda slot: numbers[5 + slot], lambda slot: numbers[5 + slots + slot]


def forward_kernel(
    numbers, own, pair, beside, across, tiles, kept, sent, rows, acc, ring, sems
):
    half = kept.shape[1]
    live, core, column, parity, height, emit_block, recv_block = unpack(numbers, tiles.shape[0])

    def prepare():
        for held, side, odd in (
            (own, column, parity),
            (pair, column, 1 - parity),
            (beside, 1 - column, parity),
            (across, 1 - column, 1 - parity),
        ):
            at = pl.ds(pl.multiple_of(side * half, half), half)
            steps = held.shape[0]
            for step in range(steps):
                rows[2 * lax.rem(height + steps - step, steps) + odd, at, :] = held[step]

    def product(slot, tile):
        return jnp.dot(tile, rows[emit_block(slot)], preferred_element_type=f32)

    sweep(live, tiles, ring, sems, prepare, product, recv_block, acc)
    mine = pl.multiple_of(core * half, half)
    other = pl.multiple_of((1 - core) * half, half)
    for block in range(kept.shape[0]):
        sent[block] = acc[block, pl.ds(other, half), :].astype(bf16)
        kept[block] = acc[block, pl.ds(mine, half), :]


def middle_kernel(terms, cotangent, w_msg, w_out, payload):
    width = w_msg.shape[0]
    pieces = terms.shape[0]
    lanes = width // 2
    summed = terms[0].astype(f32)
    for piece in range(1, pieces):
        summed += terms[piece].astype(f32)
    summed = summed.astype(bf16)
    message = jnp.dot(summed, w_msg[...], preferred_element_type=f32).astype(bf16)
    preact = jnp.dot(message, w_out[...], preferred_element_type=f32)
    sigmoid_pre = jax.nn.sigmoid(preact)
    slope = sigmoid_pre * (1.0 + preact * (1.0 - sigmoid_pre))
    grad_preact = (cotangent[...].astype(f32) * slope).astype(bf16)
    across = (((1,), (1,)), ((), ()))
    along = (((0,), (0,)), ((), ()))
    grad_turned = lax.dot_general(w_out[...], grad_preact, across, preferred_element_type=f32).astype(bf16)
    grad = lax.dot_general(grad_preact, w_out[...], across, preferred_element_type=f32).astype(bf16)
    out_part = lax.dot_general(message, grad_preact, along, preferred_element_type=f32).astype(bf16)
    msg_part = lax.dot_general(summed, grad, along, preferred_element_type=f32).astype(bf16)
    parts = (
        out_part[:, :lanes],
        out_part[:, lanes:],
        msg_part[:, :lanes],
        msg_part[:, lanes:],
    )
    chunk = 4 * width // pieces
    for piece in range(pieces):
        payload[piece, :width, :] = grad_turned
        at = 0
        while at < chunk:
            quarter, row = divmod(piece * chunk + at, width)
            size = min(chunk - at, width - row)
            payload[piece, width + at : width + at + size, :] = parts[quarter][row : row + size]
            at += size


def backward_kernel(
    numbers, held, other, tiles, own, pair, beside, across, grads, acc, ring, sems
):
    live, core, column, parity, height, emit_block, recv_block = unpack(numbers, tiles.shape[0])
    width, lanes = acc.shape[1], held.shape[2]
    steps = own.shape[0]

    def lay(first, second):
        for block in range(held.shape[0]):
            grads[block, :, :lanes] = first[block, :width, :]
            grads[block, :, lanes:] = second[block, :width, :]

    def prepare():
        @pl.when(core == 0)
        def _():
            lay(held, other)

        @pl.when(core == 1)
        def _():
            lay(other, held)

    def product(slot, tile):
        return jnp.dot(grads[recv_block(slot)], tile, preferred_element_type=f32)

    sweep(live, tiles, ring, sems, prepare, product, emit_block, acc)
    def hand_out(near):
        for out, side, odd in (
            (own, near, parity),
            (pair, near, 1 - parity),
            (beside, 1 - near, parity),
            (across, 1 - near, 1 - parity),
        ):
            for step in range(steps):
                at = 2 * lax.rem(height + step, steps) + odd
                block = acc[at, :, side * lanes : (side + 1) * lanes]
                out[step] = block.astype(bf16)

    @pl.when(column == 0)
    def _():
        hand_out(0)

    @pl.when(column == 1)
    def _():
        hand_out(1)


def copy_kernel(source, out):
    out[...] = source[...]


def chunk_kernel(held, other, second_core, out):
    chunk = out.shape[1]
    width = held.shape[1] - 2 * chunk

    def summed(rows):
        total = held[0, rows, :].astype(f32) + other[0, rows, :].astype(f32)
        for block in range(1, held.shape[0]):
            total += held[block, rows, :].astype(f32) + other[block, rows, :].astype(f32)
        return total

    first, second = summed(slice(width, width + chunk)), summed(slice(width + chunk, None))
    mine = jnp.where(second_core[0:1, :] > 0.5, second, first).astype(bf16)
    for piece in range(out.shape[0]):
        out[piece] = mine


def quad_kernel(own, pair, beside, across, *outs):
    for step, out in enumerate(outs):
        near = own[step].astype(f32) + pair[step].astype(f32)
        far = beside[step].astype(f32) + across[step].astype(f32)
        out[...] = (near + far).astype(bf16)


def weights_kernel(terms, total):
    summed = terms[0].astype(f32)
    for piece in range(1, terms.shape[0]):
        summed += terms[piece].astype(f32)
    for piece in range(total.shape[0]):
        total[piece] = summed


def result_kernel(*refs):
    terms, (w_msg, gathered, grad, grad_w_msg, grad_w_out) = refs[:-5], refs[-5:]
    lanes = gathered.shape[2]
    summed = terms[0][...].astype(f32)
    for term in terms[1:]:
        summed += term[...].astype(f32)
    grad[...] = lax.dot_general(
        summed.astype(bf16), w_msg[...], (((0,), (1,)), ((), ())), preferred_element_type=f32
    ).astype(bf16)
    for quarter, out in enumerate((grad_w_out, grad_w_out, grad_w_msg, grad_w_msg)):
        at = quarter % 2 * lanes
        out[:, at : at + lanes] = gathered[quarter]


def in_vmem(count):
    return [pl.BlockSpec(memory_space=pltpu.VMEM)] * count


def in_smem(count):
    return [pl.BlockSpec(memory_space=pltpu.SMEM)] * count


def limits(mebibytes):
    return pltpu.CompilerParams(vmem_limit_bytes=mebibytes * 2**20)


def per_device(features, cotangent, w_msg, w_out, tile_vals, tile_emit, tile_recv, tile_count):
    own_rows = features[0]
    facet_rows, width = own_rows.shape
    tile_dim = tile_vals.shape[-1]
    emit_size = lax.axis_size("emit")
    recv_size = lax.axis_size("recv")
    recv_blocks = facet_rows * emit_size // tile_dim
    emit_blocks = facet_rows * recv_size // tile_dim
    chips = emit_size // 2
    lanes = width // 2
    values = tile_vals[0, 0]
    steps = recv_size // 4
    recv_at = lax.axis_index("recv")
    column, parity = lax.rem(recv_at, 2), lax.rem(lax.div(recv_at, 2), 2)
    core = lax.rem(lax.axis_index("emit"), 2)
    numbers = jnp.concatenate(
        [
            tile_count[0],
            jnp.stack([core, column, parity, lax.div(recv_at, 4)]),
            tile_emit[0, 0],
            tile_recv[0, 0],
        ]
    )
    same_core = [list(range(parity, emit_size, 2)) for parity in range(2)]
    swap = [(member, member ^ 1) for member in range(emit_size)]
    struct = jax.ShapeDtypeStruct
    in_hbm = pl.BlockSpec(memory_space=pltpu.HBM)
    sweep_scratch = [
        pltpu.VMEM((ring_depth, group_tiles, tile_dim, tile_dim), bf16),
        pltpu.SemaphoreType.DMA((ring_depth,)),
    ]

    second_core = jnp.broadcast_to(core.astype(f32), (8, lanes))
    rated_long = pl.CostEstimate(flops=2**37, bytes_accessed=2**24, transcendentals=0)
    sweep_cost = pl.CostEstimate(
        flops=2 * values.size * width, bytes_accessed=2 * values.size, transcendentals=0
    )

    def to_quad(array, bits):
        return lax.ppermute(array, "recv", [(member, member ^ bits) for member in range(recv_size)])

    def along_z(array, step):
        return lax.ppermute(
            array, "recv", [(member, (member + 4 * step) % recv_size) for member in range(recv_size)]
        )

    arrivals = {step: along_z(own_rows, step) for step in sorted(range(1, steps), key=lambda step: abs(2 * step - steps))}
    held_rows = pl.pallas_call(
        copy_kernel,
        out_shape=struct(own_rows.shape, bf16),
        in_specs=in_vmem(1),
        out_specs=in_vmem(1)[0],
        compiler_params=limits(8),
        name="own_rows",
    )(own_rows)
    column_rows = jnp.stack([held_rows] + [arrivals[step] for step in range(1, steps)])
    kept, sent = pl.pallas_call(
        forward_kernel,
        out_shape=(
            struct((recv_blocks, tile_dim // 2, width), f32),
            struct((recv_blocks, tile_dim // 2, width), bf16),
        ),
        in_specs=in_smem(1) + in_vmem(4) + [in_hbm],
        out_specs=tuple(in_vmem(2)),
        scratch_shapes=[
            pltpu.VMEM((emit_blocks, tile_dim, width), bf16),
            pltpu.VMEM((recv_blocks + 1, tile_dim, width), f32),
        ]
        + sweep_scratch,
        compiler_params=limits(48),
        cost_estimate=sweep_cost,
        name="forward_sweep",
    )(
        numbers,
        column_rows,
        to_quad(column_rows, 2),
        to_quad(column_rows, 1),
        to_quad(column_rows, 3),
        values,
    )
    arrived = lax.ppermute(sent, "emit", swap)
    pair_sum = (kept + arrived.astype(f32)).astype(bf16)
    terms = lax.all_to_all(pair_sum, "emit", 0, 0, tiled=True, axis_index_groups=same_core)

    chunk = 4 * width // chips
    payload = pl.pallas_call(
        middle_kernel,
        out_shape=struct((chips, width + chunk, lanes), bf16),
        in_specs=in_vmem(4),
        out_specs=in_vmem(1)[0],
        compiler_params=limits(16),
        name="middle",
    )(terms, cotangent[0], w_msg, w_out)
    held = lax.all_to_all(payload, "emit", 0, 0, tiled=True, axis_index_groups=same_core)
    other = lax.ppermute(held, "emit", swap)

    weights = pl.pallas_call(
        chunk_kernel,
        out_shape=struct((recv_size, chunk // 2, lanes), bf16),
        in_specs=in_vmem(3),
        out_specs=in_vmem(1)[0],
        compiler_params=limits(8),
        name="weights_chunk",
    )(held, other, second_core)
    chunks = lax.all_to_all(weights, "recv", 0, 0, tiled=True)

    own, pair, beside, across = pl.pallas_call(
        backward_kernel,
        out_shape=(struct((steps, width, lanes), bf16),) * 4,
        in_specs=in_smem(1) + in_vmem(2) + [in_hbm],
        out_specs=tuple(in_vmem(4)),
        scratch_shapes=[
            pltpu.VMEM((recv_blocks, width, tile_dim), bf16),
            pltpu.VMEM((emit_blocks + 1, width, tile_dim), f32),
        ]
        + sweep_scratch,
        compiler_params=limits(48),
        cost_estimate=sweep_cost,
        name="backward_sweep",
    )(numbers, held, other, values)
    terms = pl.pallas_call(
        quad_kernel,
        out_shape=(struct((width, lanes), bf16),) * steps,
        in_specs=in_vmem(4),
        out_specs=tuple(in_vmem(steps)),
        compiler_params=limits(8),
        cost_estimate=rated_long,
        name="quad_sum",
    )(own, to_quad(pair, 2), to_quad(beside, 1), to_quad(across, 3))
    total = pl.pallas_call(
        weights_kernel,
        out_shape=struct((emit_size, chunk // 2, lanes), f32),
        in_specs=in_vmem(1),
        out_specs=in_vmem(1)[0],
        compiler_params=limits(8),
        name="weights_sum",
    )(chunks)
    gathered = lax.all_to_all(total, "emit", 0, 0, tiled=True).reshape(4, width, lanes)
    terms = [terms[0]] + [along_z(terms[step], step) for step in range(1, steps)]
    grad_features, grad_w_msg, grad_w_out = pl.pallas_call(
        result_kernel,
        out_shape=(
            struct((facet_rows, width), bf16),
            struct((width, width), f32),
            struct((width, width), f32),
        ),
        in_specs=in_vmem(steps + 2),
        out_specs=tuple(in_vmem(3)),
        compiler_params=limits(8),
        name="results",
    )(*terms, w_msg, gathered)
    return (grad_features[None], grad_w_msg, grad_w_out)


def solution(mesh):
    in_specs = (
        P("emit", "recv", None),
        P("recv", "emit", None),
        P(),
        P(),
        P("emit", "recv", None, None, None),
        P("emit", "recv", None),
        P("emit", "recv", None),
        P("emit", "recv"),
    )
    out_specs = (P("emit", "recv", None), P(), P())
    return jax.shard_map(
        per_device, mesh=mesh, in_specs=in_specs, out_specs=out_specs, check_vma=False
    )
```

```python
import jax
import jax.numpy as jnp
from jax import lax
from jax.experimental import pallas as pl
from jax.experimental.pallas import tpu as pltpu
from jax.sharding import PartitionSpec as P

ring_depth = 4
group_tiles = 16
f32 = jnp.float32
bf16 = jnp.bfloat16


def add_group(first, live, tiles, product, target, acc):
    spare = acc.shape[0] - 1
    slots = [first + at for at in range(group_tiles)]
    products = [product(slot, tiles[at]) for at, slot in enumerate(slots)]
    for slot, term in zip(slots, products):
        acc[jnp.where(slot < live, target(slot), spare)] += term


def sweep(live, tiles, ring, sems, prepare, product, target, acc):
    depth = ring.shape[0]
    steps = lax.div(live + group_tiles - 1, group_tiles)

    def copy(step):
        place = lax.rem(step, depth)
        return pltpu.make_async_copy(
            tiles.at[pl.ds(step * group_tiles, group_tiles)], ring.at[place], sems.at[place]
        )

    def begin(step, carry):
        copy(step).start()
        return carry

    lax.fori_loop(0, jnp.minimum(steps, depth), begin, 0)
    acc[...] = jnp.zeros_like(acc)
    prepare()

    def advance(step, carry):
        copy(step).wait()
        held = ring.at[lax.rem(step, depth)]
        add_group(step * group_tiles, live, held, product, target, acc)

        @pl.when(step + depth < steps)
        def _():
            copy(step + depth).start()

        return carry

    lax.fori_loop(0, steps, advance, 0)


def unpack(numbers, slots):
    return *(numbers[at] for at in range(5)), lambda slot: numbers[5 + slot], lambda slot: numbers[5 + slots + slot]


def forward_kernel(
    numbers, own, pair, beside, across, tiles, kept, sent, rows, acc, ring, sems
):
    half = kept.shape[1]
    live, core, column, parity, height, emit_block, recv_block = unpack(numbers, tiles.shape[0])

    def prepare():
        for held, side, odd in (
            (own, column, parity),
            (pair, column, 1 - parity),
            (beside, 1 - column, parity),
            (across, 1 - column, 1 - parity),
        ):
            at = pl.ds(pl.multiple_of(side * half, half), half)
            steps = held.shape[0]
            for step in range(steps):
                rows[2 * lax.rem(height + steps - step, steps) + odd, at, :] = held[step]

    def product(slot, tile):
        return jnp.dot(tile, rows[emit_block(slot)], preferred_element_type=f32)

    sweep(live, tiles, ring, sems, prepare, product, recv_block, acc)
    mine = pl.multiple_of(core * half, half)
    other = pl.multiple_of((1 - core) * half, half)
    for block in range(kept.shape[0]):
        sent[block] = acc[block, pl.ds(other, half), :].astype(bf16)
        kept[block] = acc[block, pl.ds(mine, half), :]


def middle_kernel(terms, cotangent, w_msg, w_out, payload):
    width = w_msg.shape[0]
    pieces = terms.shape[0]
    lanes = width // 2
    summed = terms[0].astype(f32)
    for piece in range(1, pieces):
        summed += terms[piece].astype(f32)
    summed = summed.astype(bf16)
    message = jnp.dot(summed, w_msg[...], preferred_element_type=f32).astype(bf16)
    preact = jnp.dot(message, w_out[...], preferred_element_type=f32)
    sigmoid_pre = jax.nn.sigmoid(preact)
    slope = sigmoid_pre * (1.0 + preact * (1.0 - sigmoid_pre))
    grad_preact = (cotangent[...].astype(f32) * slope).astype(bf16)
    across = (((1,), (1,)), ((), ()))
    along = (((0,), (0,)), ((), ()))
    grad_turned = lax.dot_general(w_out[...], grad_preact, across, preferred_element_type=f32).astype(bf16)
    grad = lax.dot_general(grad_preact, w_out[...], across, preferred_element_type=f32).astype(bf16)
    out_part = lax.dot_general(message, grad_preact, along, preferred_element_type=f32).astype(bf16)
    msg_part = lax.dot_general(summed, grad, along, preferred_element_type=f32).astype(bf16)
    parts = (
        out_part[:, :lanes],
        out_part[:, lanes:],
        msg_part[:, :lanes],
        msg_part[:, lanes:],
    )
    chunk = 4 * width // pieces
    for piece in range(pieces):
        payload[piece, :width, :] = grad_turned
        at = 0
        while at < chunk:
            quarter, row = divmod(piece * chunk + at, width)
            size = min(chunk - at, width - row)
            payload[piece, width + at : width + at + size, :] = parts[quarter][row : row + size]
            at += size


def backward_kernel(
    numbers, held, other, tiles, own, pair, beside, across, grads, acc, ring, sems
):
    live, core, column, parity, height, emit_block, recv_block = unpack(numbers, tiles.shape[0])
    width, lanes = acc.shape[1], held.shape[2]
    steps = own.shape[0]

    def lay(first, second):
        for block in range(held.shape[0]):
            grads[block, :, :lanes] = first[block, :width, :]
            grads[block, :, lanes:] = second[block, :width, :]

    def prepare():
        @pl.when(core == 0)
        def _():
            lay(held, other)

        @pl.when(core == 1)
        def _():
            lay(other, held)

    def product(slot, tile):
        return jnp.dot(grads[recv_block(slot)], tile, preferred_element_type=f32)

    sweep(live, tiles, ring, sems, prepare, product, emit_block, acc)
    def hand_out(near):
        for out, side, odd in (
            (own, near, parity),
            (pair, near, 1 - parity),
            (beside, 1 - near, parity),
            (across, 1 - near, 1 - parity),
        ):
            for step in range(steps):
                at = 2 * lax.rem(height + step, steps) + odd
                block = acc[at, :, side * lanes : (side + 1) * lanes]
                out[step] = block.astype(bf16)

    @pl.when(column == 0)
    def _():
        hand_out(0)

    @pl.when(column == 1)
    def _():
        hand_out(1)


def copy_kernel(source, out):
    out[...] = source[...]


def chunk_kernel(held, other, second_core, out):
    chunk = out.shape[1]
    width = held.shape[1] - 2 * chunk

    def summed(rows):
        total = held[0, rows, :].astype(f32) + other[0, rows, :].astype(f32)
        for block in range(1, held.shape[0]):
            total += held[block, rows, :].astype(f32) + other[block, rows, :].astype(f32)
        return total

    first, second = summed(slice(width, width + chunk)), summed(slice(width + chunk, None))
    mine = jnp.where(second_core[0:1, :] > 0.5, second, first).astype(bf16)
    for piece in range(out.shape[0]):
        out[piece] = mine


def quad_kernel(own, pair, beside, across, *outs):
    for step, out in enumerate(outs):
        near = own[step].astype(f32) + pair[step].astype(f32)
        far = beside[step].astype(f32) + across[step].astype(f32)
        out[...] = (near + far).astype(bf16)


def weights_kernel(terms, total):
    summed = terms[0].astype(f32)
    for piece in range(1, terms.shape[0]):
        summed += terms[piece].astype(f32)
    for piece in range(total.shape[0]):
        total[piece] = summed


def result_kernel(*refs):
    terms, (w_msg, gathered, grad, grad_w_msg, grad_w_out) = refs[:-5], refs[-5:]
    lanes = gathered.shape[2]
    summed = terms[0][...].astype(f32)
    for term in terms[1:]:
        summed += term[...].astype(f32)
    grad[...] = lax.dot_general(
        summed.astype(bf16), w_msg[...], (((0,), (1,)), ((), ())), preferred_element_type=f32
    ).astype(bf16)
    for quarter, out in enumerate((grad_w_out, grad_w_out, grad_w_msg, grad_w_msg)):
        at = quarter % 2 * lanes
        out[:, at : at + lanes] = gathered[quarter]


def in_vmem(count):
    return [pl.BlockSpec(memory_space=pltpu.VMEM)] * count


def in_smem(count):
    return [pl.BlockSpec(memory_space=pltpu.SMEM)] * count


def limits(mebibytes):
    return pltpu.CompilerParams(vmem_limit_bytes=mebibytes * 2**20)


def per_device(features, cotangent, w_msg, w_out, tile_vals, tile_emit, tile_recv, tile_count):
    own_rows = features[0]
    facet_rows, width = own_rows.shape
    tile_dim = tile_vals.shape[-1]
    emit_size = lax.axis_size("emit")
    recv_size = lax.axis_size("recv")
    recv_blocks = facet_rows * emit_size // tile_dim
    emit_blocks = facet_rows * recv_size // tile_dim
    chips = emit_size // 2
    lanes = width // 2
    values = tile_vals[0, 0]
    steps = recv_size // 4
    recv_at = lax.axis_index("recv")
    column, parity = lax.rem(recv_at, 2), lax.rem(lax.div(recv_at, 2), 2)
    core = lax.rem(lax.axis_index("emit"), 2)
    numbers = jnp.concatenate(
        [
            tile_count[0],
            jnp.stack([core, column, parity, lax.div(recv_at, 4)]),
            tile_emit[0, 0],
            tile_recv[0, 0],
        ]
    )
    same_core = [list(range(parity, emit_size, 2)) for parity in range(2)]
    swap = [(member, member ^ 1) for member in range(emit_size)]
    struct = jax.ShapeDtypeStruct
    in_hbm = pl.BlockSpec(memory_space=pltpu.HBM)
    sweep_scratch = [
        pltpu.VMEM((ring_depth, group_tiles, tile_dim, tile_dim), bf16),
        pltpu.SemaphoreType.DMA((ring_depth,)),
    ]

    second_core = jnp.broadcast_to(core.astype(f32), (8, lanes))
    rated_long = pl.CostEstimate(flops=2**37, bytes_accessed=2**24, transcendentals=0)
    sweep_cost = pl.CostEstimate(
        flops=2 * values.size * width, bytes_accessed=2 * values.size, transcendentals=0
    )

    def to_quad(array, bits):
        return lax.ppermute(array, "recv", [(member, member ^ bits) for member in range(recv_size)])

    def along_z(array, step):
        return lax.ppermute(
            array, "recv", [(member, (member + 4 * step) % recv_size) for member in range(recv_size)]
        )

    arrivals = {step: along_z(own_rows, step) for step in sorted(range(1, steps), key=lambda step: abs(2 * step - steps))}
    held_rows = pl.pallas_call(
        copy_kernel,
        out_shape=struct(own_rows.shape, bf16),
        in_specs=in_vmem(1),
        out_specs=in_vmem(1)[0],
        compiler_params=limits(8),
        name="own_rows",
    )(own_rows)
    column_rows = jnp.stack([held_rows] + [arrivals[step] for step in range(1, steps)])
    kept, sent = pl.pallas_call(
        forward_kernel,
        out_shape=(
            struct((recv_blocks, tile_dim // 2, width), f32),
            struct((recv_blocks, tile_dim // 2, width), bf16),
        ),
        in_specs=in_smem(1) + in_vmem(4) + [in_hbm],
        out_specs=tuple(in_vmem(2)),
        scratch_shapes=[
            pltpu.VMEM((emit_blocks, tile_dim, width), bf16),
            pltpu.VMEM((recv_blocks + 1, tile_dim, width), f32),
        ]
        + sweep_scratch,
        compiler_params=limits(48),
        cost_estimate=sweep_cost,
        name="forward_sweep",
    )(
        numbers,
        column_rows,
        to_quad(column_rows, 2),
        to_quad(column_rows, 1),
        to_quad(column_rows, 3),
        values,
    )
    arrived = lax.ppermute(sent, "emit", swap)
    pair_sum = (kept + arrived.astype(f32)).astype(bf16)
    terms = lax.all_to_all(pair_sum, "emit", 0, 0, tiled=True, axis_index_groups=same_core)

    chunk = 4 * width // chips
    payload = pl.pallas_call(
        middle_kernel,
        out_shape=struct((chips, width + chunk, lanes), bf16),
        in_specs=in_vmem(4),
        out_specs=in_vmem(1)[0],
        compiler_params=limits(16),
        name="middle",
    )(terms, cotangent[0], w_msg, w_out)
    held = lax.all_to_all(payload, "emit", 0, 0, tiled=True, axis_index_groups=same_core)
    other = lax.ppermute(held, "emit", swap)

    weights = pl.pallas_call(
        chunk_kernel,
        out_shape=struct((recv_size, chunk // 2, lanes), bf16),
        in_specs=in_vmem(3),
        out_specs=in_vmem(1)[0],
        compiler_params=limits(8),
        name="weights_chunk",
    )(held, other, second_core)
    chunks = lax.all_to_all(weights, "recv", 0, 0, tiled=True)

    own, pair, beside, across = pl.pallas_call(
        backward_kernel,
        out_shape=(struct((steps, width, lanes), bf16),) * 4,
        in_specs=in_smem(1) + in_vmem(2) + [in_hbm],
        out_specs=tuple(in_vmem(4)),
        scratch_shapes=[
            pltpu.VMEM((recv_blocks, width, tile_dim), bf16),
            pltpu.VMEM((emit_blocks + 1, width, tile_dim), f32),
        ]
        + sweep_scratch,
        compiler_params=limits(48),
        cost_estimate=sweep_cost,
        name="backward_sweep",
    )(numbers, held, other, values)
    terms = pl.pallas_call(
        quad_kernel,
        out_shape=(struct((width, lanes), bf16),) * steps,
        in_specs=in_vmem(4),
        out_specs=tuple(in_vmem(steps)),
        compiler_params=limits(8),
        cost_estimate=rated_long,
        name="quad_sum",
    )(own, to_quad(pair, 2), to_quad(beside, 1), to_quad(across, 3))
    total = pl.pallas_call(
        weights_kernel,
        out_shape=struct((emit_size, chunk // 2, lanes), f32),
        in_specs=in_vmem(1),
        out_specs=in_vmem(1)[0],
        compiler_params=limits(8),
        name="weights_sum",
    )(chunks)
    gathered = lax.all_to_all(total, "emit", 0, 0, tiled=True).reshape(4, width, lanes)
    terms = [terms[0]] + [along_z(terms[step], step) for step in range(1, steps)]
    grad_features, grad_w_msg, grad_w_out = pl.pallas_call(
        result_kernel,
        out_shape=(
            struct((facet_rows, width), bf16),
            struct((width, width), f32),
            struct((width, width), f32),
        ),
        in_specs=in_vmem(steps + 2),
        out_specs=tuple(in_vmem(3)),
        compiler_params=limits(8),
        name="results",
    )(*terms, w_msg, gathered)
    return (grad_features[None], grad_w_msg, grad_w_out)


def solution(mesh):
    in_specs = (
        P("emit", "recv", None),
        P("recv", "emit", None),
        P(),
        P(),
        P("emit", "recv", None, None, None),
        P("emit", "recv", None),
        P("emit", "recv", None),
        P("emit", "recv"),
    )
    out_specs = (P("emit", "recv", None), P(), P())
    return jax.shard_map(
        per_device, mesh=mesh, in_specs=in_specs, out_specs=out_specs, check_vma=False
    )
```
